256 devices in a mesh: blk: 64 (over x, z, y_hi), rows: 4 (over y_lo, core).
Axes of the slice: x: 4, y: 4 (y_hi: 2, y_lo: 2; y = y_hi * 2 + y_lo), z: 8, core: 2. Of those that a mesh axis runs over, the one named last changes fastest.
Arguments:
- features: bfloat16 [65536, 2048], P(('blk', 'rows')), may hold values from -24 to 24
- head_weight: bfloat16 [2048, 768], replicated, may hold values from -0.0048828125 to 0.0048828125
- labels: int32 [65536], P(('blk', 'rows')), may hold values from 0 to 11317
- pos_index: int32 [65536, 3], P(('blk', 'rows')), may hold values from 0 to 1023
- pair_mask: int32 [64, 3], P('blk'), may hold values from 0 to 1, as said below
- loss_weight: float32 [65536], P(('blk', 'rows')), may hold values from 0.25 to 1
Outputs:
- anchor_loss: float32 [65536], P(('blk', 'rows'))
- weight_grad: float32 [2048, 768], P(('blk', 'rows'))
The draws below stay inside these ranges and needn't reach their ends.
Inputs may be any that keep to these rules, and one draw needn't show every extreme that they name: `pair_mask`: entry [t, s] is 1 where anchor tile t scores the rows of tile (t - s) mod 64, else 0. The rows of tiles 0 to 2 and of tile 64 - 1 are all ones.
All inputs are finite; a program needn't handle non-finite values.
Results may differ from the reference program's by a relative error of at most 0.0034.
Values may be sent and summed in bfloat16 or wider, within the bound.
No kernel may reach another device: no remote copies, remote signals or barrier semaphores. Data moves between devices by JAX's collectives and lax.ppermute only.
A program may use at most 128 MiB of HBM per device.

```python
import math
import jax
import jax.numpy as jnp
import numpy as np
from jax import lax

D = 768
F = 2048
POSITIVES = 3
WIN = 2
CLASSES = 11318
BAND = 3
TILE = 1024
BATCH = 65536
N_BLK = 64


def draw_pair_mask(key, part):
    level_key, score_key = jax.random.split(jax.random.fold_in(key, 17))
    levels = jax.random.randint(level_key, (N_BLK, 1), 1, BAND + 1)
    scores = jax.random.randint(score_key, (N_BLK, BAND), 0, BAND * BAND * BAND)
    base = (scores < levels * levels * levels).astype(jnp.int32)
    tile_ids = jnp.arange(N_BLK, dtype=jnp.int32)[:, None]
    forced = (tile_ids <= WIN) | (tile_ids >= N_BLK - 1)
    return jnp.where(forced, jnp.ones_like(base), base).astype(jnp.int32)


def plant(drawn, rng, low, largest):
    shape = drawn.shape
    spot = [jax.random.randint(jax.random.fold_in(rng, axis), (), 0, shape[axis]) for axis in range(len(shape))]
    drawn = drawn.at[tuple(spot)].set(low)
    longest = shape.index(max(shape))
    spot[longest] = (spot[longest] + 1) % shape[longest]
    return drawn.at[tuple(spot)].set(largest)


def spiked(array, own_key, source, target, blocks, factor):
    def block_of(axis_at):
        return (jnp.arange(array.shape[axis_at]) // (array.shape[axis_at] // blocks)).reshape((-1,) + (1,) * (array.ndim - 1 - axis_at))

    near = jax.random.permutation(own_key, blocks)[block_of(target)]
    other_side = (block_of(target) + blocks // 2) % blocks
    return jnp.where((block_of(source) == near) | (block_of(source) == other_side), factor * array, array)


def block_scale(rng, extent, pieces, low, largest):
    gain, own = 1.0, jax.random.fold_in(rng, 6)
    for axis_at, parts in pieces:
        heights = jnp.exp(jax.random.uniform(jax.random.fold_in(own, axis_at), (parts,), jnp.float32, low / len(pieces), largest / len(pieces)))
        gain = gain * jnp.repeat(heights, extent[axis_at] // parts).reshape([-1 if axis == axis_at else 1 for axis in range(len(extent))])
    return gain


def cumulative_ranks(count, slope):
    loads = [(1 << 20) // math.isqrt(standing ** slope) + 1 for standing in range(1, count + 1)]
    spread = 1 + sum(loads) // (1 << 30)
    return np.cumsum(np.array([max(1, weight // spread) for weight in loads]))


def skewed_ids(stream_key, dims, count, skew):
    grid = cumulative_ranks(count, skew)
    pick = jax.random.randint(jax.random.fold_in(stream_key, 1), dims, 0, int(grid[count - 1]))
    standing = jnp.searchsorted(jnp.asarray(grid, jnp.int32), pick, side="right")
    return jax.random.permutation(jax.random.fold_in(stream_key, 2), count)[standing].astype(jnp.int32)


def bell_draw(own_key, shape, scale, bound, cuts=(), held_as=jnp.bfloat16):
    result = scale * jax.random.normal(own_key, shape, jnp.float32)
    if cuts:
        result = result * block_scale(own_key, shape, cuts, -0.22, 0.18)
    return jnp.clip(result, -bound, bound).astype(held_as)


def bell_draw_with(key, extent, deviation, limit, pieces, heavy, kind=jnp.bfloat16):
    values = deviation * jax.random.normal(key, extent, jnp.float32)
    if pieces:
        values = values * block_scale(key, extent, pieces, -0.22, 0.18)
    return jnp.clip(spiked(values, jax.random.fold_in(key, 3), *heavy), -limit, limit).astype(kind)


def setup_inputs(seed: int = 0) -> dict:
    arg_keys = jax.random.split(jax.random.key(seed), 7)
    features = bell_draw_with(arg_keys[0], (BATCH, F), 1.0, 24.0, ((0, 256),), (0, 1, 256, 6.0))
    head_weight = bell_draw(arg_keys[1], (F, D), (F * D) ** -0.5, 0.0048828125)
    labels = plant(skewed_ids(arg_keys[2], (BATCH,), CLASSES, 3), jax.random.fold_in(arg_keys[2], 3), 0, CLASSES - 1).astype(jnp.int32)
    pos_index = plant(jax.random.randint(arg_keys[3], (BATCH, POSITIVES), 0, TILE), jax.random.fold_in(arg_keys[3], 1), 0, TILE - 1).astype(jnp.int32)
    pair_mask = draw_pair_mask(jax.random.fold_in(arg_keys[6], 71), 0)
    loss_weight = jnp.clip(jnp.exp(math.log(1.0) - 1.3862944 * jax.random.uniform(arg_keys[5], (BATCH,), jnp.float32) ** block_scale(arg_keys[5], (BATCH,), ((0, 256),), -0.2, 0.2)), 0.25, 1.0)
    return {"features": features, "head_weight": head_weight, "labels": labels, "pos_index": pos_index, "pair_mask": pair_mask, "loss_weight": loss_weight}


SMOOTHING_SCALE = 16.0
SLACK_GAP = 0.1


def score_tile(anchors, anchor_sq, anchor_labels, matching_separation, weights, tile_rows, tile_labels, listed):
    matching_samples = matching_separation.shape[1]
    block_tally = tile_rows.shape[0]
    anchor_count = anchors.shape[0]

    def compute(unused):
        products = lax.dot_general(anchors, tile_rows, (((1,), (1,)), ((), ())), preferred_element_type=jnp.float32)
        widened = tile_rows.astype(jnp.float32)
        tile_sq = jnp.sum(widened * widened, axis=1)
        couple_separation = anchor_sq[:, None] + tile_sq[None, :] - 2.0 * products
        valid = (anchor_labels[:, None] != tile_labels[None, :]).astype(jnp.float32)
        weighting = weights / (matching_samples * block_tally)
        objective_accrued = jnp.zeros((anchor_count,), jnp.float32)
        coefficient = jnp.zeros((anchor_count, block_tally), jnp.float32)
        totals = []
        for target_slot in range(matching_samples):
            slack_excess = SMOOTHING_SCALE * (matching_separation[:, target_slot:target_slot + 1] - couple_separation + SLACK_GAP)
            objective_accrued = objective_accrued + jnp.sum(valid * jax.nn.softplus(slack_excess), axis=1)
            sigmoids = valid * jax.nn.sigmoid(slack_excess)
            coefficient = coefficient + sigmoids
            totals.append(jnp.sum(sigmoids, axis=1))
        objective_accrued = objective_accrued / (SMOOTHING_SCALE * matching_samples * block_tally)
        coefficient = coefficient * weighting[:, None]
        pos_coef = jnp.stack(totals, axis=1) * weighting[:, None]
        coef_low = coefficient.astype(jnp.bfloat16)
        anchor_grad = 2.0 * jnp.dot(coef_low, tile_rows, preferred_element_type=jnp.float32)
        pulled = lax.dot_general(coef_low, anchors, (((0,), (0,)), ((), ())), preferred_element_type=jnp.float32)
        tile_grad = 2.0 * (pulled - jnp.sum(coefficient, axis=0)[:, None] * widened)
        return objective_accrued, pos_coef, anchor_grad, tile_grad

    def skip(unused):
        return (jnp.zeros((anchor_count,), jnp.float32),
                jnp.zeros((anchor_count, matching_samples), jnp.float32),
                jnp.zeros((anchor_count, anchors.shape[1]), jnp.float32),
                jnp.zeros((block_tally, anchors.shape[1]), jnp.float32))

    return lax.cond(listed, compute, skip, 0)


def reference(features, head_weight, labels, pos_index, pair_mask, loss_weight):
    embedded = jnp.dot(features, head_weight, preferred_element_type=jnp.float32).astype(jnp.bfloat16)
    widened = embedded.astype(jnp.float32)
    squares = jnp.sum(widened * widened, axis=1)
    tile_emb = embedded.reshape(N_BLK, TILE, D)
    tile_sq = squares.reshape(N_BLK, TILE)
    tile_lab = labels.reshape(N_BLK, TILE)
    tile_pos = pos_index.reshape(N_BLK, TILE, POSITIVES)
    tile_weight = loss_weight.reshape(N_BLK, TILE)

    def per_tile(term_total, inputs):
        index, anchors, anchor_sq, anchor_labels, positions, weights, mask_row = inputs
        pos_rows = anchors[positions]
        pos_wide = pos_rows.astype(jnp.float32)
        pos_sq = anchor_sq[positions]
        matching_separation = anchor_sq[:, None] + pos_sq - 2.0 * jnp.einsum(
            "ad,akd->ak", anchors.astype(jnp.float32), pos_wide)
        loss_total = jnp.zeros((TILE,), jnp.float32)
        coef_total = jnp.zeros((TILE, POSITIVES), jnp.float32)
        grad_total = jnp.zeros((TILE, D), jnp.float32)
        for offset in range(BAND):
            target = (index - offset) % N_BLK
            tile_rows = lax.dynamic_index_in_dim(tile_emb, target, 0, keepdims=False)
            tile_labels = lax.dynamic_index_in_dim(tile_lab, target, 0, keepdims=False)
            loss_part, coef_part, grad_part, term_part = score_tile(
                anchors, anchor_sq, anchor_labels, matching_separation, weights, tile_rows, tile_labels, mask_row[offset] > 0)
            loss_total = loss_total + loss_part
            coef_total = coef_total + coef_part
            grad_total = grad_total + grad_part
            current = lax.dynamic_index_in_dim(term_total, target, 0, keepdims=False)
            term_total = lax.dynamic_update_index_in_dim(term_total, current + term_part, target, 0)
        grad_total = grad_total - 2.0 * jnp.sum(coef_total[:, :, None] * pos_wide, axis=1)
        pushed = 2.0 * coef_total[:, :, None] * (pos_wide - anchors.astype(jnp.float32)[:, None, :])
        own_term = jnp.zeros((TILE, D), jnp.float32).at[positions.reshape(-1)].add(pushed.reshape(-1, D))
        current = lax.dynamic_index_in_dim(term_total, index, 0, keepdims=False)
        term_total = lax.dynamic_update_index_in_dim(term_total, current + own_term, index, 0)
        return term_total, (loss_total, grad_total)

    start_terms = jnp.zeros((N_BLK, TILE, D), jnp.float32)
    term_total, outputs = lax.scan(per_tile, start_terms, (jnp.arange(N_BLK, dtype=jnp.int32), tile_emb, tile_sq, tile_lab, tile_pos, tile_weight, pair_mask))
    loss_tiles, grad_tiles = outputs
    emb_grad = grad_tiles.reshape(BATCH, D) + term_total.reshape(BATCH, D)
    grad_low = emb_grad.astype(jnp.bfloat16)
    weight_grad = jnp.dot(features.T, grad_low, preferred_element_type=jnp.float32)
    return loss_tiles.reshape(BATCH), weight_grad
```

```python
import functools

import jax
import jax.numpy as jnp
from jax import lax
from jax.experimental import pallas as pl
from jax.experimental.pallas import tpu as pltpu
from jax.sharding import PartitionSpec as P

SMOOTHING_SCALE = 16.0
SLACK_GAP = 0.1
LN2 = 0.6931471805599453
BASE2 = SMOOTHING_SCALE / LN2
MASKED = 1e30
META = 16
CHUNK = 16
f32 = jnp.float32
bf16 = jnp.bfloat16

VMEM = pl.BlockSpec(memory_space=pltpu.VMEM)
SMEM = pl.BlockSpec(memory_space=pltpu.SMEM)


def call(kernel, inputs, outs, scratch=(), flops=0, name=None):
    moved = sum(x.size * x.dtype.itemsize for x in inputs)
    moved += sum(x.size * x.dtype.itemsize for x in outs)
    return pl.pallas_call(
        kernel,
        out_shape=outs,
        in_specs=[SMEM if x.ndim == 1 else VMEM for x in inputs],
        out_specs=[VMEM] * len(outs),
        scratch_shapes=list(scratch),
        compiler_params=pltpu.CompilerParams(vmem_limit_bytes=40 << 20),
        cost_estimate=pl.CostEstimate(flops=flops, bytes_accessed=moved, transcendentals=0),
        name=name,
    )(*inputs)


def shape(*dims, dtype=f32):
    return jax.ShapeDtypeStruct(dims, dtype)


def nn(a, b):
    return jnp.dot(a, b, preferred_element_type=f32)


def nt(a, b):
    return lax.dot_general(a, b, (((1,), (1,)), ((), ())), preferred_element_type=f32)


def tn(a, b):
    return lax.dot_general(a, b, (((0,), (0,)), ((), ())), preferred_element_type=f32)


def embed_kernel(features_ref, weight_ref, meta_ref, out_ref):
    rows = features_ref.shape[0]
    out_ref[:rows, :] = nn(features_ref[...], weight_ref[...]).astype(bf16)
    out_ref[rows:, :] = meta_ref[...]


def score_block(
    rows_n, listed, tile, anchors_ref, labels_n, products_ref, coef_ref, lanes_ref, sq_ref, sums_ref
):
    n = rows_n.shape[0]
    wide = rows_n.astype(f32)
    squares = jnp.sum(wide * wide, axis=1, keepdims=True) * BASE2
    sq_ref[...] = jnp.broadcast_to(jnp.where(listed, squares, MASKED), sq_ref.shape)
    lanes_ref[...] = jnp.zeros_like(lanes_ref)
    for i, part in enumerate(tile):
        lanes = slice(i * n, (i + 1) * n)
        products_ref[...] = nt(rows_n, part) * (2.0 * BASE2)
        base = [anchors_ref[k : k + 1, lanes] for k in range(3)]
        weight = anchors_ref[6:7, lanes]
        labels_a = anchors_ref[7:8, lanes]

        def step(c, carry, lanes=lanes, base=base, weight=weight, labels_a=labels_a):
            at = pl.multiple_of(c * CHUNK, CHUNK)
            rows = pl.ds(at, CHUNK)
            q = sq_ref[rows, :1] - products_ref[rows, :]
            q = jnp.where(labels_n[rows, :1] == labels_a, MASKED, q)
            y = [b - q for b in base]
            e = [jnp.exp2(-jnp.abs(v)) for v in y]
            a = [1.0 + v for v in e]
            a01 = a[0] * a[1]
            excess = e[0] + e[1] * a[0] + e[2] * a01
            total = 1.0 + excess
            inverse = 1.0 / total
            log_sum = jnp.log(total) + (excess - (total - 1.0))
            tops = jnp.maximum(y[0], 0.0) + jnp.maximum(y[1], 0.0) + jnp.maximum(y[2], 0.0)
            loss = tops * LN2 + log_sum
            inv2 = inverse * a[2]
            s = [inv2 * a[1], inv2 * a[0], inverse * a01]
            s = [v * jnp.where(w >= 0.0, 1.0, x) for v, w, x in zip(s, y, e)]
            coef = (s[0] + s[1] + s[2]) * weight
            coef_ref[rows, lanes] = coef.astype(bf16)
            folded = coef[:, :128]
            for j in range(128, n, 128):
                folded = folded + coef[:, j : j + 128]
            lanes_ref[rows, :] += folded
            fold = lambda v: jnp.sum(v.reshape(CHUNK // 8, 8, n), axis=0)
            return tuple(x + fold(v) for x, v in zip(carry, (*s, loss)))

        zero = jnp.zeros((8, n), f32)
        sums = lax.fori_loop(0, n // CHUNK, step, (zero,) * 4)
        for k, v in enumerate(sums):
            sums_ref[k : k + 1, lanes] += jnp.sum(v, axis=0, keepdims=True)


def negative_grad(rows_n, tile, coef_ref, lanes_ref):
    n = rows_n.shape[0]
    pulled = sum(nn(coef_ref[:, i * n : (i + 1) * n], part) for i, part in enumerate(tile))
    col_sums = jnp.sum(lanes_ref[...], axis=1, keepdims=True)
    return 2.0 * (pulled - col_sums * rows_n.astype(f32))


def column(row):
    n = row.shape[1]
    eye = lax.broadcasted_iota(jnp.int32, (n, n), 0) == lax.broadcasted_iota(jnp.int32, (n, n), 1)
    return jnp.sum(jnp.where(eye, jnp.broadcast_to(row, (n, n)), 0.0), axis=1, keepdims=True)


def meta_row(ref, n, i):
    return ref[n : n + META, :n].astype(f32)[i : i + 1, :]


def own_kernel(
    scal_ref, p0, p1, p2, p3, anchors_ref, coef_ref, sums_ref, grad_ref,
    products_ref, lanes_ref, sq_ref, label_ref,
):
    blocks = (p0, p1, p2, p3)
    n = p0.shape[0] - META
    me = scal_ref[0]
    scale = 1.0 / (3 * 4 * n)
    tile = [p[:n, :] for p in blocks]
    squares = []
    for part in tile:
        wide = part.astype(f32)
        squares.append(jnp.sum(wide * wide, axis=1, keepdims=True))
    for i, p in enumerate(blocks):
        lanes = slice(i * n, (i + 1) * n)
        meta = p[n : n + META, :n].astype(f32)
        where = []
        for k in range(3):
            holder = meta[2 + k : 3 + k, :].astype(jnp.int32) ^ me
            where.append(holder * n + meta[5 + k : 6 + k, :].astype(jnp.int32))
        found = [jnp.zeros((1, n), f32) for _ in range(3)]
        for j, part in enumerate(tile):
            apart = squares[j] - 2.0 * nt(part, tile[i])
            index = lax.broadcasted_iota(jnp.int32, (n, n), 0) + j * n
            for k in range(3):
                picked = jnp.where(index == where[k], apart, 0.0)
                found[k] = found[k] + jnp.sum(picked, axis=0, keepdims=True)
        for k in range(3):
            anchors_ref[k : k + 1, lanes] = (found[k] + SLACK_GAP) * BASE2
            anchors_ref[3 + k : 4 + k, lanes] = where[k].astype(f32)
        weight = meta[8:9, :] + meta[9:10, :] + meta[10:11, :]
        anchors_ref[6:7, lanes] = weight * scale
        anchors_ref[7:8, lanes] = meta[0:1, :] * 128.0 + meta[1:2, :]
    label_ref[...] = jnp.broadcast_to(column(anchors_ref[7:8, :n]), label_ref.shape)
    sums_ref[...] = jnp.zeros_like(sums_ref)
    score_block(
        tile[0], scal_ref[1] > 0, tile, anchors_ref, label_ref, products_ref, coef_ref, lanes_ref,
        sq_ref, sums_ref,
    )
    grad_ref[...] = negative_grad(tile[0], tile, coef_ref, lanes_ref)


def earlier_kernel(
    scal_ref, n1, n2, p0, p1, p2, p3, anchors_ref, before_ref, coef1, coef2, sums_ref, grad1, grad2,
    products_ref, lanes_ref, sq_ref, label_ref,
):
    n = p0.shape[0] - META
    tile = [p[:n, :] for p in (p0, p1, p2, p3)]
    sums_ref[...] = before_ref[...]
    for s, (p, coef_ref, grad_ref) in enumerate(((n1, coef1, grad1), (n2, coef2, grad2))):
        labels = meta_row(p, n, 0) * 128.0 + meta_row(p, n, 1)
        label_ref[...] = jnp.broadcast_to(column(labels), label_ref.shape)
        rows_n = p[:n, :]
        score_block(
            rows_n, scal_ref[2 + s] > 0, tile, anchors_ref, label_ref, products_ref, coef_ref,
            lanes_ref, sq_ref, sums_ref,
        )
        grad_ref[...] = negative_grad(rows_n, tile, coef_ref, lanes_ref).astype(bf16)
    weight = anchors_ref[6:7, :]
    for k in range(3):
        sums_ref[k : k + 1, :] = sums_ref[k : k + 1, :] * weight


def anchor_kernel(c0, c1, c2, n0, n1, n2, keep_ref, send_ref):
    n = n0.shape[0] - META
    for i, (ref, j) in enumerate(((keep_ref, 0), (send_ref, 0), (keep_ref, 1), (send_ref, 1))):
        lanes = slice(i * n, (i + 1) * n)
        total = tn(c0[:, lanes], n0[:n, :])
        total = total + tn(c1[:, lanes], n1[:n, :]) + tn(c2[:, lanes], n2[:n, :])
        ref[j * n : (j + 1) * n, :] = 2.0 * total


def listed_kernel(anchors_ref, coef_ref, own_where, own_coef, p0, p1, p2, p3, base_ref, out_ref):
    n = p0.shape[0] - META
    tile = [p[:n, :] for p in (p0, p1, p2, p3)]
    total = jnp.zeros(out_ref.shape, f32)
    pushed = jnp.zeros((n, 1), f32)
    for i, part in enumerate(tile):
        lanes = slice(i * n, (i + 1) * n)
        mine = lax.broadcasted_iota(jnp.int32, (n, n), 0).astype(f32)
        others = (lax.broadcasted_iota(jnp.int32, (n, n), 1) + i * n).astype(f32)
        matrix = jnp.zeros((n, n), f32)
        for k in range(3):
            hit = anchors_ref[3 + k : 4 + k, lanes] == mine
            matrix = matrix + jnp.where(hit, coef_ref[k : k + 1, lanes], 0.0)
        pushed = pushed + jnp.sum(matrix, axis=1, keepdims=True)
        for k in range(3):
            hit = own_where[:, k : k + 1] == others
            matrix = matrix + jnp.where(hit, own_coef[:, k : k + 1], 0.0)
        high = matrix.astype(bf16)
        low = (matrix - high.astype(f32)).astype(bf16)
        total = total + nn(high, part) + nn(low, part)
    out_ref[...] = base_ref[...] + 2.0 * (pushed * tile[0].astype(f32) - total)


def head_kernel(f0, f2, f13, g0, g1, g2, g3, out_ref):
    m = f0.shape[0]
    total = nn(f0[...], g0[...]) + nn(f13[:m, :], g1[...])
    total = total + nn(f2[...], g2[...]) + nn(f13[m:, :], g3[...])
    out_ref[...] = total.astype(bf16)


def local(features, head_weight, labels, pos_index, pair_mask, loss_weight):
    blks, rows_n = lax.axis_size("blk"), lax.axis_size("rows")
    me = lax.axis_index("rows")
    n, depth = features.shape
    wide = head_weight.shape[1]
    slice_rows = depth // (blks * rows_n)

    def over_rows(x, flip):
        return lax.ppermute(x, "rows", [(i, i ^ flip) for i in range(rows_n)])

    def over_blk(x, by):
        return lax.ppermute(x, "blk", [(i, (i + by) % blks) for i in range(blks)])

    pos = pos_index.T
    w_hi = loss_weight.astype(bf16).astype(f32)
    w_mid = (loss_weight - w_hi).astype(bf16).astype(f32)
    meta = jnp.concatenate(
        [
            (labels >> 7)[None].astype(bf16),
            (labels & 127)[None].astype(bf16),
            (pos // n).astype(bf16),
            (pos % n).astype(bf16),
            w_hi[None].astype(bf16),
            w_mid[None].astype(bf16),
            (loss_weight - w_hi - w_mid)[None].astype(bf16),
        ]
    )
    meta = jnp.pad(meta, ((0, META - meta.shape[0]), (0, wide - n)))
    (p0,) = call(
        embed_kernel,
        (features, head_weight, meta),
        [shape(n + META, wide, dtype=bf16)],
        flops=2 * n * depth * wide,
        name="embed",
    )
    p2 = over_rows(p0, 2)
    n1, n2 = over_blk(p0, 1), over_blk(p0, 2)
    p1 = over_rows(p0, 1)
    p3 = over_rows(p2, 1)

    turned = features.T.reshape(blks, rows_n, slice_rows, n)
    turned = [
        lax.dynamic_index_in_dim(turned, me ^ j, 1, keepdims=False).reshape(blks * slice_rows, n)
        for j in range(4)
    ]
    f2 = over_rows(jnp.concatenate(turned[2:]), 2)
    m = blks * slice_rows
    f13 = over_rows(jnp.concatenate([turned[1], f2[m:]]), 1)
    f2 = f2[:m]

    scal = jnp.concatenate([me[None].astype(jnp.int32), pair_mask[0]])
    scratch = [
        pltpu.VMEM((n, n), f32),
        pltpu.VMEM((n, 128), f32),
        pltpu.VMEM((n, 128), f32),
        pltpu.VMEM((n, 128), f32),
    ]
    tile = (p0, p1, p2, p3)
    anchors, c0, sums, own_grad = call(
        own_kernel,
        (scal, *tile),
        [shape(8, 4 * n), shape(n, 4 * n, dtype=bf16), shape(8, 4 * n), shape(n, wide)],
        scratch,
        flops=2 * n * n * wide * 40,
        name="own_block",
    )
    c1, c2, sums, grad1, grad2 = call(
        earlier_kernel,
        (scal, n1, n2, *tile, anchors, sums),
        [
            shape(n, 4 * n, dtype=bf16),
            shape(n, 4 * n, dtype=bf16),
            shape(8, 4 * n),
            shape(n, wide, dtype=bf16),
            shape(n, wide, dtype=bf16),
        ],
        scratch,
        flops=2 * n * n * wide * 40,
        name="earlier_blocks",
    )
    grad1, grad2 = over_blk(grad1, -1), over_blk(grad2, -2)
    keep, send = call(
        anchor_kernel,
        (c0, c1, c2, p0, n1, n2),
        [shape(2 * n, wide), shape(2 * n, wide)],
        flops=2 * n * n * wide * 12,
        name="anchor_grad",
    )
    half = keep + over_rows(send, 1)
    from_y = over_rows(half[n:].astype(bf16), 2)

    other = over_rows(sums, 1).reshape(8, 2, 2, n)[:, :, ::-1].reshape(8, 4 * n)
    sums = sums + other
    other = over_rows(sums, 2).reshape(8, 2, 2 * n)[:, ::-1].reshape(8, 4 * n)
    sums = sums + other
    anchor_loss = sums[3, :n] / (SMOOTHING_SCALE * 3 * 4 * n)
    own_where = (((pos_index // n) ^ me) * n + pos_index % n).astype(f32)
    (base,) = call(
        listed_kernel,
        (anchors, sums, own_where, sums[:, :n].T, *tile, half[:n] + own_grad),
        [shape(n, wide)],
        flops=2 * n * n * wide * 8,
        name="listed",
    )
    total = base + from_y.astype(f32) + grad1.astype(f32) + grad2.astype(f32)
    g0 = total.astype(bf16)
    g2 = over_rows(g0, 2)
    g1 = over_rows(g0, 1)
    g3 = over_rows(g2, 1)
    (part,) = call(
        head_kernel,
        (turned[0], f2, f13, g0, g1, g2, g3),
        [shape(m, wide, dtype=bf16)],
        flops=2 * m * 4 * n * wide,
        name="head_grad",
    )
    parts = lax.all_to_all(part, "blk", split_axis=0, concat_axis=0, tiled=True)
    weight_grad = jnp.sum(parts.reshape(blks, slice_rows, wide).astype(f32), axis=0)
    return anchor_loss, weight_grad


def solution(mesh):
    return jax.shard_map(
        local,
        mesh=mesh,
        in_specs=(
            P(("blk", "rows"), None),
            P(),
            P(("blk", "rows")),
            P(("blk", "rows"), None),
            P("blk", None),
            P(("blk", "rows")),
        ),
        out_specs=(P(("blk", "rows")), P(("blk", "rows"), None)),
        check_vma=False,
    )
```

```python
import functools

import jax
import jax.numpy as jnp
from jax import lax
from jax.experimental import pallas as pl
from jax.experimental.pallas import tpu as pltpu
from jax.sharding import PartitionSpec as P

SMOOTHING_SCALE = 16.0
SLACK_GAP = 0.1
LN2 = 0.6931471805599453
BASE2 = SMOOTHING_SCALE / LN2
MASKED = 1e30
META = 16
OWN_US = 3.0
CHUNK = 16
f32 = jnp.float32
bf16 = jnp.bfloat16

VMEM = pl.BlockSpec(memory_space=pltpu.VMEM)
SMEM = pl.BlockSpec(memory_space=pltpu.SMEM)


def call(kernel, inputs, outs, scratch=(), micros=0.0, name=None):
    return pl.pallas_call(
        kernel,
        out_shape=outs,
        in_specs=[SMEM if x.ndim == 1 else VMEM for x in inputs],
        out_specs=[VMEM] * len(outs),
        scratch_shapes=list(scratch),
        compiler_params=pltpu.CompilerParams(vmem_limit_bytes=16 << 20),
        cost_estimate=pl.CostEstimate(
            flops=int(micros * 1.15e9), bytes_accessed=1024, transcendentals=0
        ),
        name=name,
    )(*inputs)


def shape(*dims, dtype=f32):
    return jax.ShapeDtypeStruct(dims, dtype)


def nn(a, b):
    return jnp.dot(a, b, preferred_element_type=f32)


def nt(a, b):
    return lax.dot_general(a, b, (((1,), (1,)), ((), ())), preferred_element_type=f32)


def tn(a, b):
    return lax.dot_general(a, b, (((0,), (0,)), ((), ())), preferred_element_type=f32)


def embed_kernel(features_ref, weight_ref, labels_ref, pos_ref, loss_weight_ref, out_ref):
    n, width = features_ref.shape[0], weight_ref.shape[1]
    out_ref[:n, :] = nn(features_ref[...], weight_ref[...]).astype(bf16)
    out_ref[n:, :] = jnp.zeros((META, width), bf16)

    @pl.when(pl.program_id(0) == 0)
    def _():
        labels, pos, weight = labels_ref[...], pos_ref[...], loss_weight_ref[...]
        high = weight.astype(bf16).astype(f32)
        middle = (weight - high).astype(bf16).astype(f32)
        rows = [labels >> 7, labels & 127, pos // n, pos % n]
        rows = [x.astype(f32) for x in rows] + [high, middle, weight - high - middle]
        rows.append(jnp.zeros((META - 11, n), f32))
        out_ref[n:, :n] = jnp.concatenate(rows, axis=0).astype(bf16)


def embed(features, head_weight, labels, pos, loss_weight):
    n, depth = features.shape
    wide, step = head_weight.shape[1], n
    return pl.pallas_call(
        embed_kernel,
        grid=(wide // step,),
        out_shape=shape(n + META, wide, dtype=bf16),
        in_specs=[
            pl.BlockSpec((n, depth), lambda i: (0, 0)),
            pl.BlockSpec((depth, step), lambda i: (0, i)),
            pl.BlockSpec((1, n), lambda i: (0, 0)),
            pl.BlockSpec((3, n), lambda i: (0, 0)),
            pl.BlockSpec((1, n), lambda i: (0, 0)),
        ],
        out_specs=pl.BlockSpec((n + META, step), lambda i: (0, i)),
        compiler_params=pltpu.CompilerParams(vmem_limit_bytes=56 << 20),
        cost_estimate=pl.CostEstimate(flops=1 << 30, bytes_accessed=1 << 22, transcendentals=0),
        name="embed",
    )(features, head_weight, labels, pos, loss_weight)


def across(x, width):
    return jnp.concatenate([x] * (width // x.shape[1]), axis=1)


def score_block(
    rows_n, listed, tile, anchors_ref, labels_n, products_ref, coef_ref, lanes_ref, sq_ref,
    sums_ref,
):
    n = rows_n.shape[0]
    wide = rows_n.astype(f32)
    squares = jnp.sum(wide * wide, axis=1, keepdims=True) * BASE2
    sq_ref[...] = jnp.broadcast_to(jnp.where(listed, squares, MASKED), sq_ref.shape)
    lanes_ref[...] = jnp.zeros_like(lanes_ref)
    for i, part in enumerate(tile):
        lanes = slice(i * n, (i + 1) * n)
        products_ref[...] = nt(rows_n, part) * (2.0 * BASE2)
        base = [anchors_ref[k : k + 1, lanes] for k in range(3)]
        weight = anchors_ref[6:7, lanes]
        labels_a = anchors_ref[7:8, lanes]

        def step(c, carry, lanes=lanes, base=base, weight=weight, labels_a=labels_a):
            at = pl.multiple_of(c * CHUNK, CHUNK)
            rows = pl.ds(at, CHUNK)
            q = across(sq_ref[rows, :], n) - products_ref[rows, :]
            q = jnp.where(across(labels_n[rows, :], n) == labels_a, MASKED, q)
            y = [b - q for b in base]
            e = [jnp.exp2(-jnp.abs(v)) for v in y]
            a = [1.0 + v for v in e]
            a01 = a[0] * a[1]
            excess = e[0] + e[1] * a[0] + e[2] * a01
            total = 1.0 + excess
            inverse = 1.0 / total
            log_sum = jnp.log(total) + (excess - (total - 1.0))
            tops = jnp.maximum(y[0], 0.0) + jnp.maximum(y[1], 0.0) + jnp.maximum(y[2], 0.0)
            loss = tops * LN2 + log_sum
            inv2 = inverse * a[2]
            s = [inv2 * a[1], inv2 * a[0], inverse * a01]
            s = [v * jnp.where(w >= 0.0, 1.0, x) for v, w, x in zip(s, y, e)]
            coef = (s[0] + s[1] + s[2]) * weight
            coef_ref[rows, lanes] = coef.astype(bf16)
            folded = coef[:, :128]
            for j in range(128, n, 128):
                folded = folded + coef[:, j : j + 128]
            lanes_ref[rows, :] += folded
            fold = lambda v: jnp.sum(v.reshape(CHUNK // 8, 8, n), axis=0)
            return tuple(x + fold(v) for x, v in zip(carry, (*s, loss)))

        zero = jnp.zeros((8, n), f32)
        sums = lax.fori_loop(0, n // CHUNK, step, (zero,) * 4, unroll=4)
        for k, v in enumerate(sums):
            sums_ref[k : k + 1, lanes] += jnp.sum(v, axis=0, keepdims=True)


def negative_grad(rows_n, tile, coef_ref, lanes_ref):
    n = rows_n.shape[0]
    pulled = sum(nn(coef_ref[:, i * n : (i + 1) * n], part) for i, part in enumerate(tile))
    col_sums = jnp.sum(lanes_ref[...], axis=1, keepdims=True)
    return 2.0 * (pulled - col_sums * rows_n.astype(f32))


def column(row):
    n = row.shape[1]
    eye = lax.broadcasted_iota(jnp.int32, (n, n), 0) == lax.broadcasted_iota(jnp.int32, (n, n), 1)
    return jnp.sum(jnp.where(eye, jnp.broadcast_to(row, (n, n)), 0.0), axis=1, keepdims=True)


def meta_row(ref, n, i):
    return ref[n : n + META, :n].astype(f32)[i : i + 1, :]


def own_kernel(
    scal_ref, p0, p1, p2, p3, anchors_ref, coef_ref, sums_ref, grad_ref,
    products_ref, lanes_ref, sq_ref, label_ref,
):
    blocks = (p0, p1, p2, p3)
    n = p0.shape[0] - META
    me = scal_ref[0]
    scale = 1.0 / (3 * 4 * n)
    tile = [p[:n, :] for p in blocks]
    squares = []
    for part in tile:
        wide = part.astype(f32)
        squares.append(jnp.sum(wide * wide, axis=1, keepdims=True))
    for i, p in enumerate(blocks):
        lanes = slice(i * n, (i + 1) * n)
        meta = p[n : n + META, :n].astype(f32)
        where = []
        for k in range(3):
            holder = meta[2 + k : 3 + k, :].astype(jnp.int32) ^ me
            where.append(holder * n + meta[5 + k : 6 + k, :].astype(jnp.int32))
        found = [jnp.zeros((1, n), f32) for _ in range(3)]
        for j, part in enumerate(tile):
            apart = squares[j] - 2.0 * nt(part, tile[i])
            index = lax.broadcasted_iota(jnp.int32, (n, n), 0) + j * n
            for k in range(3):
                picked = jnp.where(index == where[k], apart, 0.0)
                found[k] = found[k] + jnp.sum(picked, axis=0, keepdims=True)
        for k in range(3):
            anchors_ref[k : k + 1, lanes] = (found[k] + SLACK_GAP) * BASE2
            anchors_ref[3 + k : 4 + k, lanes] = where[k].astype(f32)
        weight = meta[8:9, :] + meta[9:10, :] + meta[10:11, :]
        anchors_ref[6:7, lanes] = weight * scale
        anchors_ref[7:8, lanes] = meta[0:1, :] * 128.0 + meta[1:2, :]
    label_ref[...] = jnp.broadcast_to(column(anchors_ref[7:8, :n]), label_ref.shape)
    sums_ref[...] = jnp.zeros_like(sums_ref)
    score_block(
        tile[0], scal_ref[1] > 0, tile, anchors_ref, label_ref, products_ref, coef_ref, lanes_ref,
        sq_ref, sums_ref,
    )
    grad_ref[...] = negative_grad(tile[0], tile, coef_ref, lanes_ref)


def earlier_kernel(
    scal_ref, n1, n2, p0, p1, p2, p3, anchors_ref, before_ref, coef1, coef2, sums_ref, grad1, grad2,
    products_ref, lanes_ref, sq_ref, label_ref,
):
    n = p0.shape[0] - META
    tile = [p[:n, :] for p in (p0, p1, p2, p3)]
    sums_ref[...] = before_ref[...]
    for s, (p, coef_ref, grad_ref) in enumerate(((n1, coef1, grad1), (n2, coef2, grad2))):
        labels = meta_row(p, n, 0) * 128.0 + meta_row(p, n, 1)
        label_ref[...] = jnp.broadcast_to(column(labels), label_ref.shape)
        rows_n = p[:n, :]
        score_block(
            rows_n, scal_ref[2 + s] > 0, tile, anchors_ref, label_ref, products_ref, coef_ref,
            lanes_ref, sq_ref, sums_ref,
        )
        grad_ref[...] = negative_grad(rows_n, tile, coef_ref, lanes_ref).astype(bf16)
    weight = anchors_ref[6:7, :]
    for k in range(3):
        sums_ref[k : k + 1, :] = sums_ref[k : k + 1, :] * weight


def anchor_kernel(first, c0, c1, c2, n0, n1, n2, keep_ref, send_ref):
    n = n0.shape[0] - META
    for i, ref in ((first, keep_ref), (first + 1, send_ref)):
        lanes = slice(i * n, (i + 1) * n)
        total = tn(c0[:, lanes], n0[:n, :])
        total = total + tn(c1[:, lanes], n1[:n, :]) + tn(c2[:, lanes], n2[:n, :])
        ref[...] = 2.0 * total


def halved_kernel(keep_ref, other_ref, out_ref):
    out_ref[...] = (keep_ref[...] + other_ref[...]).astype(bf16)


def listed_kernel(
    anchors_ref, s0, s1, s2, s3, p0, p1, p2, p3, keep_ref, other_ref, own_ref, out_ref, loss_ref
):
    n = p0.shape[0] - META
    tile = [p[:n, :] for p in (p0, p1, p2, p3)]
    sums = []
    for i in range(4):
        parts = [s[:, (i ^ j) * n : ((i ^ j) + 1) * n] for j, s in enumerate((s0, s1, s2, s3))]
        sums.append((parts[0] + parts[1]) + (parts[2] + parts[3]))
    loss_ref[...] = sums[0][3:4, :] * (1.0 / (SMOOTHING_SCALE * 3 * 4 * n))
    own_coef = [column(sums[0][k : k + 1, :]) for k in range(3)]
    own_where = [column(anchors_ref[3 + k : 4 + k, :n]) for k in range(3)]
    total = jnp.zeros(out_ref.shape, f32)
    pushed = jnp.zeros((n, 1), f32)
    for i, part in enumerate(tile):
        lanes = slice(i * n, (i + 1) * n)
        mine = lax.broadcasted_iota(jnp.int32, (n, n), 0).astype(f32)
        others = (lax.broadcasted_iota(jnp.int32, (n, n), 1) + i * n).astype(f32)
        matrix = jnp.zeros((n, n), f32)
        for k in range(3):
            hit = anchors_ref[3 + k : 4 + k, lanes] == mine
            matrix = matrix + jnp.where(hit, sums[i][k : k + 1, :], 0.0)
        pushed = pushed + jnp.sum(matrix, axis=1, keepdims=True)
        for k in range(3):
            matrix = matrix + jnp.where(own_where[k] == others, own_coef[k], 0.0)
        high = matrix.astype(bf16)
        low = (matrix - high.astype(f32)).astype(bf16)
        total = total + nn(high, part) + nn(low, part)
    base = keep_ref[...] + other_ref[...] + own_ref[...]
    out_ref[...] = base + 2.0 * (pushed * tile[0].astype(f32) - total)


def gathered_kernel(base_ref, y_ref, one_ref, two_ref, out_ref):
    total = base_ref[...] + y_ref[...].astype(f32)
    out_ref[...] = (total + (one_ref[...].astype(f32) + two_ref[...].astype(f32))).astype(bf16)


def head_kernel(f0, f1, f2, f3, g0, g1, g2, g3, out_ref):
    total = nn(f0[...], g0[...]) + nn(f1[...], g1[...])
    total = total + nn(f2[...], g2[...]) + nn(f3[...], g3[...])
    out_ref[...] = total.astype(bf16)


def local(features, head_weight, labels, pos_index, pair_mask, loss_weight):
    blks, rows_n = lax.axis_size("blk"), lax.axis_size("rows")
    me = lax.axis_index("rows")
    n, depth = features.shape
    wide = head_weight.shape[1]
    slice_rows = depth // (blks * rows_n)

    def over_rows(x, flip):
        return lax.ppermute(x, "rows", [(i, i ^ flip) for i in range(rows_n)])

    def along(x, by, flip):
        pairs = [
            (b * rows_n + i, (b + by) % blks * rows_n + (i ^ flip))
            for b in range(blks)
            for i in range(rows_n)
        ]
        return lax.ppermute(x, ("blk", "rows"), pairs)

    p0 = embed(features, head_weight, labels[None], pos_index.T, loss_weight[None])
    p2 = over_rows(p0, 2)
    n1, n2 = along(p0, 1, 2), along(p0, 2, 0)
    p1 = over_rows(p0, 1)

    features, _ = lax.optimization_barrier((features, p0))
    m = blks * slice_rows
    turned = features.T.reshape(blks, rows_n, slice_rows, n)
    turned = [
        lax.dynamic_index_in_dim(turned, me ^ j, 1, keepdims=False).reshape(m, n) for j in range(4)
    ]
    f0 = turned[0]
    p2, *turned = lax.optimization_barrier((p2, *turned))
    p3 = over_rows(p2, 1)
    f1 = over_rows(turned[1], 1)
    f2, f3 = over_rows(turned[2], 2), over_rows(turned[3], 2)

    scal = jnp.concatenate([me[None].astype(jnp.int32), pair_mask[0]])
    scratch = [pltpu.VMEM((n, n), f32)] + [pltpu.VMEM((n, 128), f32)] * 3
    tile = (p0, p1, p2, p3)
    low_grad = shape(n, wide, dtype=bf16)
    low_coef = shape(n, 4 * n, dtype=bf16)
    anchors, c0, sums, own_grad = call(
        own_kernel,
        (scal, *tile),
        [shape(8, 4 * n), low_coef, shape(8, 4 * n), shape(n, wide)],
        scratch,
        micros=OWN_US, name="own_block",
    )
    f2, f3, sums = lax.optimization_barrier((f2, f3, sums))
    f3 = over_rows(f3, 1)
    c1, c2, s0, grad1, grad2 = call(
        earlier_kernel,
        (scal, n1, n2, *tile, anchors, sums),
        [low_coef, low_coef, shape(8, 4 * n), low_grad, low_grad],
        scratch,
        micros=8.0, name="earlier_blocks",
    )
    s1, s2 = over_rows(s0, 1), over_rows(s0, 2)
    grad1, grad2 = along(grad1, -1, 2), along(grad2, -2, 0)
    pieces = (c0, c1, c2, p0, n1, n2)
    rows_f32 = [shape(n, wide), shape(n, wide)]
    keep, send = call(
        functools.partial(anchor_kernel, 2), pieces, rows_f32, micros=1.3, name="anchor_grad_across"
    )
    (half,) = call(halved_kernel, (keep, over_rows(send, 1)), [low_grad], micros=0.5, name="half_sum")
    from_y = over_rows(half, 2)
    keep, send = call(functools.partial(anchor_kernel, 0), pieces, rows_f32, micros=1.3, name="anchor_grad_own")
    s3 = over_rows(s2, 1)
    base, anchor_loss = call(
        listed_kernel,
        (anchors, s0, s1, s2, s3, *tile, keep, over_rows(send, 1), own_grad),
        [shape(n, wide), shape(1, n)],
        micros=2.0, name="listed",
    )
    (g0,) = call(gathered_kernel, (base, from_y, grad1, grad2), [low_grad], micros=0.7, name="row_grad")
    g2 = over_rows(g0, 2)
    g1 = over_rows(g0, 1)
    g3 = over_rows(g2, 1)
    (part,) = call(
        head_kernel,
        (f0, f1, f2, f3, g0, g1, g2, g3),
        [shape(m, wide, dtype=bf16)],
        micros=1.5, name="head_grad",
    )
    parts = lax.all_to_all(part, "blk", split_axis=0, concat_axis=0, tiled=True)
    weight_grad = jnp.sum(parts.reshape(blks, slice_rows, wide).astype(f32), axis=0)
    return anchor_loss[0], weight_grad


def solution(mesh):
    return jax.shard_map(
        local,
        mesh=mesh,
        in_specs=(
            P(("blk", "rows"), None),
            P(),
            P(("blk", "rows")),
            P(("blk", "rows"), None),
            P("blk", None),
            P(("blk", "rows")),
        ),
        out_specs=(P(("blk", "rows")), P(("blk", "rows"), None)),
        check_vma=False,
    )
```

```python
import functools

import jax
import jax.numpy as jnp
from jax import lax
from jax.experimental import pallas as pl
from jax.experimental.pallas import tpu as pltpu
from jax.sharding import PartitionSpec as P

SMOOTHING_SCALE = 16.0
SLACK_GAP = 0.1
LN2 = 0.6931471805599453
BASE2 = SMOOTHING_SCALE / LN2
MASKED = 1e30
META = 16
CHUNK = 16
f32 = jnp.float32
bf16 = jnp.bfloat16

VMEM = pl.BlockSpec(memory_space=pltpu.VMEM)
SMEM = pl.BlockSpec(memory_space=pltpu.SMEM)


def call(kernel, inputs, outs, scratch=(), micros=0.0, name=None):
    return pl.pallas_call(
        kernel,
        out_shape=outs,
        in_specs=[SMEM if x.ndim == 1 else VMEM for x in inputs],
        out_specs=[VMEM] * len(outs),
        scratch_shapes=list(scratch),
        compiler_params=pltpu.CompilerParams(vmem_limit_bytes=16 << 20),
        cost_estimate=pl.CostEstimate(
            flops=int(micros * 1.15e9), bytes_accessed=1024, transcendentals=0
        ),
        name=name,
    )(*inputs)


def shape(*dims, dtype=f32):
    return jax.ShapeDtypeStruct(dims, dtype)


def nn(a, b):
    return jnp.dot(a, b, preferred_element_type=f32)


def nt(a, b):
    return lax.dot_general(a, b, (((1,), (1,)), ((), ())), preferred_element_type=f32)


def tn(a, b):
    return lax.dot_general(a, b, (((0,), (0,)), ((), ())), preferred_element_type=f32)


def embed_kernel(features_ref, weight_ref, labels_ref, pos_ref, loss_weight_ref, out_ref):
    n, width = features_ref.shape[0], weight_ref.shape[1]
    out_ref[:n, :] = nn(features_ref[...], weight_ref[...]).astype(bf16)
    out_ref[n:, :] = jnp.zeros((META, width), bf16)

    @pl.when(pl.program_id(0) == 0)
    def _():
        labels, pos, weight = labels_ref[...], pos_ref[...], loss_weight_ref[...]
        high = weight.astype(bf16).astype(f32)
        middle = (weight - high).astype(bf16).astype(f32)
        rows = [labels >> 7, labels & 127, pos // n, pos % n]
        rows = [x.astype(f32) for x in rows] + [high, middle, weight - high - middle]
        rows.append(jnp.zeros((META - 11, n), f32))
        out_ref[n:, :n] = jnp.concatenate(rows, axis=0).astype(bf16)


def embed(features, head_weight, labels, pos, loss_weight):
    n, depth = features.shape
    wide = head_weight.shape[1]
    step = wide // 2
    return pl.pallas_call(
        embed_kernel,
        grid=(wide // step,),
        out_shape=shape(n + META, wide, dtype=bf16),
        in_specs=[
            pl.BlockSpec((n, depth), lambda i: (0, 0)),
            pl.BlockSpec((depth, step), lambda i: (0, i)),
            pl.BlockSpec((1, n), lambda i: (0, 0)),
            pl.BlockSpec((3, n), lambda i: (0, 0)),
            pl.BlockSpec((1, n), lambda i: (0, 0)),
        ],
        out_specs=pl.BlockSpec((n + META, step), lambda i: (0, i)),
        compiler_params=pltpu.CompilerParams(vmem_limit_bytes=56 << 20),
        cost_estimate=pl.CostEstimate(flops=1 << 30, bytes_accessed=1 << 22, transcendentals=0),
        name="embed",
    )(features, head_weight, labels, pos, loss_weight)


def across(x, width):
    return jnp.concatenate([x] * (width // x.shape[1]), axis=1)


def score_block(
    rows_n, listed, tile, anchors_ref, labels_n, products_ref, coef_ref, lanes_ref, sq_ref,
    sums_ref,
):
    n = rows_n.shape[0]
    wide = rows_n.astype(f32)
    squares = jnp.sum(wide * wide, axis=1, keepdims=True) * BASE2
    sq_ref[...] = jnp.broadcast_to(jnp.where(listed, squares, MASKED), sq_ref.shape)
    lanes_ref[...] = jnp.zeros_like(lanes_ref)
    for i, part in enumerate(tile):
        lanes = slice(i * n, (i + 1) * n)
        products_ref[...] = nt(rows_n, part) * (2.0 * BASE2)
        base = [anchors_ref[k : k + 1, lanes] for k in range(3)]
        weight = anchors_ref[6:7, lanes]
        labels_a = anchors_ref[7:8, lanes]

        def step(c, carry, lanes=lanes, base=base, weight=weight, labels_a=labels_a):
            at = pl.multiple_of(c * CHUNK, CHUNK)
            rows = pl.ds(at, CHUNK)
            q = across(sq_ref[rows, :], n) - products_ref[rows, :]
            q = jnp.where(across(labels_n[rows, :], n) == labels_a, MASKED, q)
            y = [b - q for b in base]
            e = [jnp.exp2(-jnp.abs(v)) for v in y]
            a = [1.0 + v for v in e]
            a01 = a[0] * a[1]
            excess = e[0] + e[1] * a[0] + e[2] * a01
            total = 1.0 + excess
            inverse = 1.0 / total
            log_sum = jnp.log(total) + (excess - (total - 1.0))
            tops = jnp.maximum(y[0], 0.0) + jnp.maximum(y[1], 0.0) + jnp.maximum(y[2], 0.0)
            loss = tops * LN2 + log_sum
            inv2 = inverse * a[2]
            s = [inv2 * a[1], inv2 * a[0], inverse * a01]
            s = [v * jnp.where(w >= 0.0, 1.0, x) for v, w, x in zip(s, y, e)]
            coef = (s[0] + s[1] + s[2]) * weight
            coef_ref[rows, lanes] = coef.astype(bf16)
            folded = coef[:, :128]
            for j in range(128, n, 128):
                folded = folded + coef[:, j : j + 128]
            lanes_ref[rows, :] += folded
            fold = lambda v: jnp.sum(v.reshape(CHUNK // 8, 8, n), axis=0)
            return tuple(x + fold(v) for x, v in zip(carry, (*s, loss)))

        zero = jnp.zeros((8, n), f32)
        sums = lax.fori_loop(0, n // CHUNK, step, (zero,) * 4, unroll=4)
        for k, v in enumerate(sums):
            sums_ref[k : k + 1, lanes] += jnp.sum(v, axis=0, keepdims=True)


def negative_grad(rows_n, tile, coef_ref, lanes_ref):
    n = rows_n.shape[0]
    pulled = sum(nn(coef_ref[:, i * n : (i + 1) * n], part) for i, part in enumerate(tile))
    col_sums = jnp.sum(lanes_ref[...], axis=1, keepdims=True)
    return 2.0 * (pulled - col_sums * rows_n.astype(f32))


def column(row):
    n = row.shape[1]
    eye = lax.broadcasted_iota(jnp.int32, (n, n), 0) == lax.broadcasted_iota(jnp.int32, (n, n), 1)
    return jnp.sum(jnp.where(eye, jnp.broadcast_to(row, (n, n)), 0.0), axis=1, keepdims=True)


def meta_row(ref, n, i):
    return ref[n : n + META, :n].astype(f32)[i : i + 1, :]


def score_kernel(
    scal_ref, p0, p1, p2, p3, n1, n2, anchors_ref, c0, c1, c2, sums_ref, grad0, grad1, grad2,
    products_ref, lanes_ref, sq_ref, label_ref,
):
    blocks = (p0, p1, p2, p3)
    n = p0.shape[0] - META
    me = scal_ref[0]
    scale = 1.0 / (3 * 4 * n)
    tile = [p[:n, :] for p in blocks]
    squares = []
    for part in tile:
        wide = part.astype(f32)
        squares.append(jnp.sum(wide * wide, axis=1, keepdims=True))
    for i, p in enumerate(blocks):
        lanes = slice(i * n, (i + 1) * n)
        meta = p[n : n + META, :n].astype(f32)
        where = []
        for k in range(3):
            holder = meta[2 + k : 3 + k, :].astype(jnp.int32) ^ me
            where.append(holder * n + meta[5 + k : 6 + k, :].astype(jnp.int32))
        found = [jnp.zeros((1, n), f32) for _ in range(3)]
        for j, part in enumerate(tile):
            apart = squares[j] - 2.0 * nt(part, tile[i])
            index = lax.broadcasted_iota(jnp.int32, (n, n), 0) + j * n
            for k in range(3):
                picked = jnp.where(index == where[k], apart, 0.0)
                found[k] = found[k] + jnp.sum(picked, axis=0, keepdims=True)
        for k in range(3):
            anchors_ref[k : k + 1, lanes] = (found[k] + SLACK_GAP) * BASE2
            anchors_ref[3 + k : 4 + k, lanes] = where[k].astype(f32)
        weight = meta[8:9, :] + meta[9:10, :] + meta[10:11, :]
        anchors_ref[6:7, lanes] = weight * scale
        anchors_ref[7:8, lanes] = meta[0:1, :] * 128.0 + meta[1:2, :]
    sums_ref[...] = jnp.zeros_like(sums_ref)
    negatives = ((p0, c0, grad0), (n1, c1, grad1), (n2, c2, grad2))
    for offset, (p, coef_ref, grad_ref) in enumerate(negatives):
        labels = meta_row(p, n, 0) * 128.0 + meta_row(p, n, 1)
        label_ref[...] = jnp.broadcast_to(column(labels), label_ref.shape)
        rows_n = p[:n, :]
        score_block(
            rows_n, scal_ref[1 + offset] > 0, tile, anchors_ref, label_ref, products_ref, coef_ref,
            lanes_ref, sq_ref, sums_ref,
        )
        grad = negative_grad(rows_n, tile, coef_ref, lanes_ref)
        grad_ref[...] = grad.astype(grad_ref.dtype)
    for k in range(3):
        sums_ref[k : k + 1, :] = sums_ref[k : k + 1, :] * anchors_ref[6:7, :]


def anchor_kernel(first, c0, c1, c2, n0, n1, n2, keep_ref, send_ref):
    n = n0.shape[0] - META
    for i, ref in ((first, keep_ref), (first + 1, send_ref)):
        lanes = slice(i * n, (i + 1) * n)
        total = tn(c0[:, lanes], n0[:n, :])
        total = total + tn(c1[:, lanes], n1[:n, :]) + tn(c2[:, lanes], n2[:n, :])
        ref[...] = 2.0 * total


def halved_kernel(keep_ref, other_ref, out_ref):
    out_ref[...] = (keep_ref[...] + other_ref[...]).astype(bf16)


def listed_kernel(
    anchors_ref, s0, s1, s2, s3, p0, p1, p2, p3, keep_ref, other_ref, own_ref, out_ref, loss_ref
):
    n = p0.shape[0] - META
    tile = [p[:n, :] for p in (p0, p1, p2, p3)]
    sums = []
    for i in range(4):
        parts = [s[:, (i ^ j) * n : ((i ^ j) + 1) * n] for j, s in enumerate((s0, s1, s2, s3))]
        sums.append((parts[0] + parts[1]) + (parts[2] + parts[3]))
    loss_ref[...] = sums[0][3:4, :] * (1.0 / (SMOOTHING_SCALE * 3 * 4 * n))
    own_coef = [column(sums[0][k : k + 1, :]) for k in range(3)]
    own_where = [column(anchors_ref[3 + k : 4 + k, :n]) for k in range(3)]
    total = jnp.zeros(out_ref.shape, f32)
    pushed = jnp.zeros((n, 1), f32)
    for i, part in enumerate(tile):
        lanes = slice(i * n, (i + 1) * n)
        mine = lax.broadcasted_iota(jnp.int32, (n, n), 0).astype(f32)
        others = (lax.broadcasted_iota(jnp.int32, (n, n), 1) + i * n).astype(f32)
        matrix = jnp.zeros((n, n), f32)
        for k in range(3):
            hit = anchors_ref[3 + k : 4 + k, lanes] == mine
            matrix = matrix + jnp.where(hit, sums[i][k : k + 1, :], 0.0)
        pushed = pushed + jnp.sum(matrix, axis=1, keepdims=True)
        for k in range(3):
            matrix = matrix + jnp.where(own_where[k] == others, own_coef[k], 0.0)
        high = matrix.astype(bf16)
        low = (matrix - high.astype(f32)).astype(bf16)
        total = total + nn(high, part) + nn(low, part)
    base = keep_ref[...] + other_ref[...] + own_ref[...]
    out_ref[...] = base + 2.0 * (pushed * tile[0].astype(f32) - total)


def gathered_kernel(base_ref, y_ref, one_ref, two_ref, out_ref):
    total = base_ref[...] + y_ref[...].astype(f32)
    out_ref[...] = (total + (one_ref[...].astype(f32) + two_ref[...].astype(f32))).astype(bf16)


def head_kernel(f0, f1, f2, f3, g0, g1, g2, g3, out_ref):
    total = nn(f0[...], g0[...]) + nn(f1[...], g1[...])
    total = total + nn(f2[...], g2[...]) + nn(f3[...], g3[...])
    out_ref[...] = total.astype(bf16)


def local(features, head_weight, labels, pos_index, pair_mask, loss_weight):
    blks, rows_n = lax.axis_size("blk"), lax.axis_size("rows")
    me = lax.axis_index("rows")
    n, depth = features.shape
    wide = head_weight.shape[1]
    slice_rows = depth // (blks * rows_n)

    def over_rows(x, flip):
        return lax.ppermute(x, "rows", [(i, i ^ flip) for i in range(rows_n)])

    def along(x, by, flip):
        pairs = [
            (b * rows_n + i, (b + by) % blks * rows_n + (i ^ flip))
            for b in range(blks)
            for i in range(rows_n)
        ]
        return lax.ppermute(x, ("blk", "rows"), pairs)

    p0 = embed(features, head_weight, labels[None], pos_index.T, loss_weight[None])
    p2 = over_rows(p0, 2)
    n1, n2 = along(p0, 1, 2), along(p0, 2, 0)
    p1 = over_rows(p0, 1)

    features, _ = lax.optimization_barrier((features, p0))
    m = blks * slice_rows
    turned = features.T.reshape(blks, rows_n, slice_rows, n)
    turned = [
        lax.dynamic_index_in_dim(turned, me ^ j, 1, keepdims=False).reshape(m, n) for j in range(4)
    ]
    f0 = turned[0]
    p2, *turned = lax.optimization_barrier((p2, *turned))
    p3 = over_rows(p2, 1)
    f1 = over_rows(turned[1], 1)
    f2, f3 = over_rows(turned[2], 2), over_rows(turned[3], 2)

    scal = jnp.concatenate([me[None].astype(jnp.int32), pair_mask[0]])
    scratch = [pltpu.VMEM((n, n), f32)] + [pltpu.VMEM((n, 128), f32)] * 3
    tile = (p0, p1, p2, p3)
    low_grad = shape(n, wide, dtype=bf16)
    low_coef = shape(n, 4 * n, dtype=bf16)
    anchors, c0, c1, c2, s0, own_grad, grad1, grad2 = call(
        score_kernel,
        (scal, *tile, n1, n2),
        [shape(8, 4 * n)] + [low_coef] * 3 + [shape(8, 4 * n), shape(n, wide)] + [low_grad] * 2,
        scratch,
        micros=14.0,
        name="score",
    )
    c0, f2, f3 = lax.optimization_barrier((c0, f2, f3))
    s2 = over_rows(s0, 2)
    s1 = over_rows(s0, 1)
    pieces = (c0, c1, c2, p0, n1, n2)
    rows_f32 = [shape(n, wide), shape(n, wide)]
    keep, send = call(
        functools.partial(anchor_kernel, 2), pieces, rows_f32, micros=1.3, name="anchor_grad_across"
    )
    keep, f1 = lax.optimization_barrier((keep, f1))
    c0, s2 = lax.optimization_barrier((c0, s2))
    (half,) = call(
        halved_kernel, (keep, over_rows(send, 1)), [low_grad], micros=0.5, name="half_sum"
    )
    half, grad1, grad2 = lax.optimization_barrier((half, grad1, grad2))
    from_y = over_rows(half, 2)
    grad1, grad2 = along(grad1, -1, 2), along(grad2, -2, 0)
    f3, s3 = over_rows(f3, 1), over_rows(s2, 1)
    keep, send = call(
        functools.partial(anchor_kernel, 0), (c0, *pieces[1:]), rows_f32, micros=1.3, name="anchor_grad_own"
    )
    s1, s3, f3 = lax.optimization_barrier((s1, s3, f3))
    base, anchor_loss = call(
        listed_kernel,
        (anchors, s0, s1, s2, s3, *tile, keep, over_rows(send, 1), own_grad),
        [shape(n, wide), shape(1, n)],
        micros=2.0,
        name="listed",
    )
    (g0,) = call(
        gathered_kernel, (base, from_y, grad1, grad2), [low_grad], micros=0.7, name="row_grad"
    )
    g2 = over_rows(g0, 2)
    g1 = over_rows(g0, 1)
    g3 = over_rows(g2, 1)
    (part,) = call(
        head_kernel,
        (f0, f1, f2, f3, g0, g1, g2, g3),
        [shape(m, wide, dtype=bf16)],
        micros=1.5, name="head_grad",
    )
    parts = lax.all_to_all(part, "blk", split_axis=0, concat_axis=0, tiled=True)
    weight_grad = jnp.sum(parts.reshape(blks, slice_rows, wide).astype(f32), axis=0)
    return anchor_loss[0], weight_grad


def solution(mesh):
    return jax.shard_map(
        local,
        mesh=mesh,
        in_specs=(
            P(("blk", "rows"), None),
            P(),
            P(("blk", "rows")),
            P(("blk", "rows"), None),
            P("blk", None),
            P(("blk", "rows")),
        ),
        out_specs=(P(("blk", "rows")), P(("blk", "rows"), None)),
        check_vma=False,
    )
```

```python
import functools

import jax
import jax.numpy as jnp
from jax import lax
from jax.experimental import pallas as pl
from jax.experimental.pallas import tpu as pltpu
from jax.sharding import PartitionSpec as P

SMOOTHING_SCALE = 16.0
SLACK_GAP = 0.1
LN2 = 0.6931471805599453
BASE2 = SMOOTHING_SCALE / LN2
MASKED = 1e30
META = 16
CHUNK = 16
f32 = jnp.float32
bf16 = jnp.bfloat16

VMEM = pl.BlockSpec(memory_space=pltpu.VMEM)
SMEM = pl.BlockSpec(memory_space=pltpu.SMEM)


def call(kernel, inputs, outs, scratch=(), micros=0.01, name=None):
    return pl.pallas_call(
        kernel,
        out_shape=outs,
        in_specs=[SMEM if x.ndim == 1 else VMEM for x in inputs],
        out_specs=[VMEM] * len(outs),
        scratch_shapes=list(scratch),
        compiler_params=pltpu.CompilerParams(vmem_limit_bytes=16 << 20),
        cost_estimate=pl.CostEstimate(
            flops=int(micros * 1.15e9), bytes_accessed=1024, transcendentals=0
        ),
        name=name,
    )(*inputs)


def shape(*dims, dtype=f32):
    return jax.ShapeDtypeStruct(dims, dtype)


def nn(a, b):
    return jnp.dot(a, b, preferred_element_type=f32)


def nt(a, b):
    return lax.dot_general(a, b, (((1,), (1,)), ((), ())), preferred_element_type=f32)


def tn(a, b):
    return lax.dot_general(a, b, (((0,), (0,)), ((), ())), preferred_element_type=f32)


def embed_kernel(features_ref, weight_ref, labels_ref, pos_ref, loss_weight_ref, out_ref):
    n, width = features_ref.shape[0], weight_ref.shape[1]
    out_ref[:n, :] = nn(features_ref[...], weight_ref[...]).astype(bf16)
    out_ref[n:, :] = jnp.zeros((META, width), bf16)

    @pl.when(pl.program_id(0) == 0)
    def _():
        labels, pos, weight = labels_ref[...], pos_ref[...], loss_weight_ref[...]
        high = weight.astype(bf16).astype(f32)
        middle = (weight - high).astype(bf16).astype(f32)
        rows = [labels >> 7, labels & 127, pos // n, pos % n]
        rows = [x.astype(f32) for x in rows] + [high, middle, weight - high - middle]
        rows.append(jnp.zeros((META - 11, n), f32))
        out_ref[n:, :n] = jnp.concatenate(rows, axis=0).astype(bf16)


def embed(features, head_weight, labels, pos, loss_weight):
    n, depth = features.shape
    wide = head_weight.shape[1]
    step = wide // 2
    return pl.pallas_call(
        embed_kernel,
        grid=(wide // step,),
        out_shape=shape(n + META, wide, dtype=bf16),
        in_specs=[
            pl.BlockSpec((n, depth), lambda i: (0, 0)),
            pl.BlockSpec((depth, step), lambda i: (0, i)),
            pl.BlockSpec((1, n), lambda i: (0, 0)),
            pl.BlockSpec((3, n), lambda i: (0, 0)),
            pl.BlockSpec((1, n), lambda i: (0, 0)),
        ],
        out_specs=pl.BlockSpec((n + META, step), lambda i: (0, i)),
        compiler_params=pltpu.CompilerParams(vmem_limit_bytes=56 << 20),
        cost_estimate=pl.CostEstimate(flops=1 << 30, bytes_accessed=1 << 22, transcendentals=0),
        name="embed",
    )(features, head_weight, labels, pos, loss_weight)


def across(x, width):
    return jnp.concatenate([x] * (width // x.shape[1]), axis=1)


def score_block(
    rows_n, listed, tile, anchors_ref, labels_n, products_ref, coef_ref, lanes_ref, sq_ref,
    sums_ref,
):
    n = rows_n.shape[0]
    wide = rows_n.astype(f32)
    squares = jnp.sum(wide * wide, axis=1, keepdims=True) * BASE2
    sq_ref[...] = jnp.broadcast_to(jnp.where(listed, squares, MASKED), sq_ref.shape)
    lanes_ref[...] = jnp.zeros_like(lanes_ref)
    for i, part in enumerate(tile):
        lanes = slice(i * n, (i + 1) * n)
        products_ref[...] = nt(rows_n, part) * (2.0 * BASE2)
        base = [anchors_ref[k : k + 1, lanes] for k in range(3)]
        weight = anchors_ref[6:7, lanes]
        labels_a = anchors_ref[7:8, lanes]

        def step(c, carry, lanes=lanes, base=base, weight=weight, labels_a=labels_a):
            at = pl.multiple_of(c * CHUNK, CHUNK)
            rows = pl.ds(at, CHUNK)
            q = across(sq_ref[rows, :], n) - products_ref[rows, :]
            q = jnp.where(across(labels_n[rows, :], n) == labels_a, MASKED, q)
            y = [b - q for b in base]
            e = [jnp.exp2(-jnp.abs(v)) for v in y]
            a = [1.0 + v for v in e]
            a01 = a[0] * a[1]
            excess = e[0] + e[1] * a[0] + e[2] * a01
            total = 1.0 + excess
            inverse = 1.0 / total
            log_sum = jnp.log(total) + (excess - (total - 1.0))
            tops = jnp.maximum(y[0], 0.0) + jnp.maximum(y[1], 0.0) + jnp.maximum(y[2], 0.0)
            loss = tops * LN2 + log_sum
            inv2 = inverse * a[2]
            s = [inv2 * a[1], inv2 * a[0], inverse * a01]
            s = [v * jnp.where(w >= 0.0, 1.0, x) for v, w, x in zip(s, y, e)]
            coef = (s[0] + s[1] + s[2]) * weight
            coef_ref[rows, lanes] = coef.astype(bf16)
            folded = coef[:, :128]
            for j in range(128, n, 128):
                folded = folded + coef[:, j : j + 128]
            lanes_ref[rows, :] += folded
            fold = lambda v: jnp.sum(v.reshape(CHUNK // 8, 8, n), axis=0)
            return tuple(x + fold(v) for x, v in zip(carry, (*s, loss)))

        zero = jnp.zeros((8, n), f32)
        sums = lax.fori_loop(0, n // CHUNK, step, (zero,) * 4, unroll=4)
        for k, v in enumerate(sums):
            sums_ref[k : k + 1, lanes] += jnp.sum(v, axis=0, keepdims=True)


def negative_grad(rows_n, tile, coef_ref, lanes_ref):
    n = rows_n.shape[0]
    pulled = sum(nn(coef_ref[:, i * n : (i + 1) * n], part) for i, part in enumerate(tile))
    col_sums = jnp.sum(lanes_ref[...], axis=1, keepdims=True)
    return 2.0 * (pulled - col_sums * rows_n.astype(f32))


def column(row):
    n = row.shape[1]
    eye = lax.broadcasted_iota(jnp.int32, (n, n), 0) == lax.broadcasted_iota(jnp.int32, (n, n), 1)
    return jnp.sum(jnp.where(eye, jnp.broadcast_to(row, (n, n)), 0.0), axis=1, keepdims=True)


def meta_row(ref, n, i):
    return ref[n : n + META, :n].astype(f32)[i : i + 1, :]


def score_kernel(
    scal_ref, p0, p1, p2, p3, n1, n2, anchors_ref, c0, c1, c2, sums_ref, grad0, grad1, grad2,
    products_ref, lanes_ref, sq_ref, label_ref,
):
    blocks = (p0, p1, p2, p3)
    n = p0.shape[0] - META
    me = scal_ref[0]
    scale = 1.0 / (3 * 4 * n)
    tile = [p[:n, :] for p in blocks]
    squares = []
    for part in tile:
        wide = part.astype(f32)
        squares.append(jnp.sum(wide * wide, axis=1, keepdims=True))
    for i, p in enumerate(blocks):
        lanes = slice(i * n, (i + 1) * n)
        meta = p[n : n + META, :n].astype(f32)
        where = []
        for k in range(3):
            holder = meta[2 + k : 3 + k, :].astype(jnp.int32) ^ me
            where.append(holder * n + meta[5 + k : 6 + k, :].astype(jnp.int32))
        found = [jnp.zeros((1, n), f32) for _ in range(3)]
        for j, part in enumerate(tile):
            apart = squares[j] - 2.0 * nt(part, tile[i])
            index = lax.broadcasted_iota(jnp.int32, (n, n), 0) + j * n
            for k in range(3):
                picked = jnp.where(index == where[k], apart, 0.0)
                found[k] = found[k] + jnp.sum(picked, axis=0, keepdims=True)
        for k in range(3):
            anchors_ref[k : k + 1, lanes] = (found[k] + SLACK_GAP) * BASE2
            anchors_ref[3 + k : 4 + k, lanes] = where[k].astype(f32)
        weight = meta[8:9, :] + meta[9:10, :] + meta[10:11, :]
        anchors_ref[6:7, lanes] = weight * scale
        anchors_ref[7:8, lanes] = meta[0:1, :] * 128.0 + meta[1:2, :]
    sums_ref[...] = jnp.zeros_like(sums_ref)
    negatives = ((p0, c0, grad0), (n1, c1, grad1), (n2, c2, grad2))
    for offset, (p, coef_ref, grad_ref) in enumerate(negatives):
        labels = meta_row(p, n, 0) * 128.0 + meta_row(p, n, 1)
        label_ref[...] = jnp.broadcast_to(column(labels), label_ref.shape)
        rows_n = p[:n, :]
        score_block(
            rows_n, scal_ref[1 + offset] > 0, tile, anchors_ref, label_ref, products_ref, coef_ref,
            lanes_ref, sq_ref, sums_ref,
        )
        grad = negative_grad(rows_n, tile, coef_ref, lanes_ref)
        grad_ref[...] = grad.astype(grad_ref.dtype)
    for k in range(3):
        sums_ref[k : k + 1, :] = sums_ref[k : k + 1, :] * anchors_ref[6:7, :]


def anchor_kernel(first, c0, c1, c2, n0, n1, n2, keep_ref, send_ref):
    n = n0.shape[0] - META
    for i, ref in ((first, keep_ref), (first + 1, send_ref)):
        lanes = slice(i * n, (i + 1) * n)
        total = tn(c0[:, lanes], n0[:n, :])
        total = total + tn(c1[:, lanes], n1[:n, :]) + tn(c2[:, lanes], n2[:n, :])
        ref[...] = 2.0 * total


def halved_kernel(keep_ref, other_ref, out_ref):
    out_ref[...] = (keep_ref[...] + other_ref[...]).astype(bf16)


def listed_kernel(
    anchors_ref, s0, s1, s2, s3, p0, p1, p2, p3, keep_ref, other_ref, own_ref, out_ref, loss_ref
):
    n = p0.shape[0] - META
    tile = [p[:n, :] for p in (p0, p1, p2, p3)]
    sums = []
    for i in range(4):
        parts = [s[:, (i ^ j) * n : ((i ^ j) + 1) * n] for j, s in enumerate((s0, s1, s2, s3))]
        sums.append((parts[0] + parts[1]) + (parts[2] + parts[3]))
    loss_ref[...] = sums[0][3:4, :] * (1.0 / (SMOOTHING_SCALE * 3 * 4 * n))
    own_coef = [column(sums[0][k : k + 1, :]) for k in range(3)]
    own_where = [column(anchors_ref[3 + k : 4 + k, :n]) for k in range(3)]
    total = jnp.zeros(out_ref.shape, f32)
    pushed = jnp.zeros((n, 1), f32)
    for i, part in enumerate(tile):
        lanes = slice(i * n, (i + 1) * n)
        mine = lax.broadcasted_iota(jnp.int32, (n, n), 0).astype(f32)
        others = (lax.broadcasted_iota(jnp.int32, (n, n), 1) + i * n).astype(f32)
        matrix = jnp.zeros((n, n), f32)
        for k in range(3):
            hit = anchors_ref[3 + k : 4 + k, lanes] == mine
            matrix = matrix + jnp.where(hit, sums[i][k : k + 1, :], 0.0)
        pushed = pushed + jnp.sum(matrix, axis=1, keepdims=True)
        for k in range(3):
            matrix = matrix + jnp.where(own_where[k] == others, own_coef[k], 0.0)
        high = matrix.astype(bf16)
        low = (matrix - high.astype(f32)).astype(bf16)
        total = total + nn(high, part) + nn(low, part)
    base = keep_ref[...] + other_ref[...] + own_ref[...]
    out_ref[...] = base + 2.0 * (pushed * tile[0].astype(f32) - total)


def gathered_kernel(base_ref, y_ref, one_ref, two_ref, out_ref):
    total = base_ref[...] + y_ref[...].astype(f32)
    out_ref[...] = (total + (one_ref[...].astype(f32) + two_ref[...].astype(f32))).astype(bf16)


def head_kernel(f0, f1, f2, f3, g0, g1, g2, g3, out_ref):
    total = nn(f0[...], g0[...]) + nn(f1[...], g1[...])
    total = total + nn(f2[...], g2[...]) + nn(f3[...], g3[...])
    out_ref[...] = total.astype(bf16)


def local(features, head_weight, labels, pos_index, pair_mask, loss_weight):
    blks, rows_n = lax.axis_size("blk"), lax.axis_size("rows")
    me = lax.axis_index("rows")
    n, depth = features.shape
    wide = head_weight.shape[1]
    slice_rows = depth // (blks * rows_n)

    def over_rows(x, flip):
        return lax.ppermute(x, "rows", [(i, i ^ flip) for i in range(rows_n)])

    def along(x, by, flip):
        pairs = [
            (b * rows_n + i, (b + by) % blks * rows_n + (i ^ flip))
            for b in range(blks)
            for i in range(rows_n)
        ]
        return lax.ppermute(x, ("blk", "rows"), pairs)

    p0 = embed(features, head_weight, labels[None], pos_index.T, loss_weight[None])
    p2 = over_rows(p0, 2)
    n1, n2 = along(p0, 1, 2), along(p0, 2, 0)
    p1 = over_rows(p0, 1)

    features, _ = lax.optimization_barrier((features, p0))
    m = blks * slice_rows
    turned = features.T.reshape(blks, rows_n, slice_rows, n)
    turned = [
        lax.dynamic_index_in_dim(turned, me ^ j, 1, keepdims=False).reshape(m, n) for j in range(4)
    ]
    f0 = turned[0]
    p2, *turned = lax.optimization_barrier((p2, *turned))
    p3 = over_rows(p2, 1)
    f1 = over_rows(turned[1], 1)
    f2, f3 = over_rows(turned[2], 2), over_rows(turned[3], 2)

    scal = jnp.concatenate([me[None].astype(jnp.int32), pair_mask[0]])
    scratch = [pltpu.VMEM((n, n), f32)] + [pltpu.VMEM((n, 128), f32)] * 3
    tile = (p0, p1, p2, p3)
    low_grad = shape(n, wide, dtype=bf16)
    low_coef = shape(n, 4 * n, dtype=bf16)
    anchors, c0, c1, c2, s0, own_grad, grad1, grad2 = call(
        score_kernel,
        (scal, *tile, n1, n2),
        [shape(8, 4 * n)] + [low_coef] * 3 + [shape(8, 4 * n), shape(n, wide)] + [low_grad] * 2,
        scratch,
        micros=0.01,
        name="score",
    )
    c0, f2, f3 = lax.optimization_barrier((c0, f2, f3))
    s2 = over_rows(s0, 2)
    s1 = over_rows(s0, 1)
    pieces = (c0, c1, c2, p0, n1, n2)
    rows_f32 = [shape(n, wide), shape(n, wide)]
    keep, send = call(
        functools.partial(anchor_kernel, 2), pieces, rows_f32, micros=0.01, name="anchor_grad_across"
    )
    keep, f1, s2 = lax.optimization_barrier((keep, f1, s2))
    (half,) = call(
        halved_kernel, (keep, over_rows(send, 1)), [low_grad], micros=0.01, name="half_sum"
    )
    from_y = over_rows(half, 2)
    grad1, grad2 = along(grad1, -1, 2), along(grad2, -2, 0)
    f3, s3 = over_rows(f3, 1), over_rows(s2, 1)
    keep, send = call(
        functools.partial(anchor_kernel, 0), pieces, rows_f32, micros=0.01, name="anchor_grad_own"
    )
    s1, s3, f3 = lax.optimization_barrier((s1, s3, f3))
    base, anchor_loss = call(
        listed_kernel,
        (anchors, s0, s1, s2, s3, *tile, keep, over_rows(send, 1), own_grad),
        [shape(n, wide), shape(1, n)],
        micros=0.01,
        name="listed",
    )
    (g0,) = call(
        gathered_kernel, (base, from_y, grad1, grad2), [low_grad], micros=0.01, name="row_grad"
    )
    g2 = over_rows(g0, 2)
    g1 = over_rows(g0, 1)
    g3 = over_rows(g2, 1)
    (part,) = call(
        head_kernel,
        (f0, f1, f2, f3, g0, g1, g2, g3),
        [shape(m, wide, dtype=bf16)],
        micros=0.01, name="head_grad",
    )
    parts = lax.all_to_all(part, "blk", split_axis=0, concat_axis=0, tiled=True)
    weight_grad = jnp.sum(parts.reshape(blks, slice_rows, wide).astype(f32), axis=0)
    return anchor_loss[0], weight_grad


def solution(mesh):
    return jax.shard_map(
        local,
        mesh=mesh,
        in_specs=(
            P(("blk", "rows"), None),
            P(),
            P(("blk", "rows")),
            P(("blk", "rows"), None),
            P("blk", None),
            P(("blk", "rows")),
        ),
        out_specs=(P(("blk", "rows")), P(("blk", "rows"), None)),
        check_vma=False,
    )
```

```python
import functools

import jax
import jax.numpy as jnp
from jax import lax
from jax.experimental import pallas as pl
from jax.experimental.pallas import tpu as pltpu
from jax.sharding import PartitionSpec as P

SMOOTHING_SCALE = 16.0
SLACK_GAP = 0.1
LN2 = 0.6931471805599453
BASE2 = SMOOTHING_SCALE / LN2
MASKED = 1e30
META = 16
CHUNK = 16
f32 = jnp.float32
bf16 = jnp.bfloat16

VMEM = pl.BlockSpec(memory_space=pltpu.VMEM)
SMEM = pl.BlockSpec(memory_space=pltpu.SMEM)


def call(kernel, inputs, outs, scratch=(), micros=0.01, name=None):
    return pl.pallas_call(
        kernel,
        out_shape=outs,
        in_specs=[SMEM if x.ndim == 1 else VMEM for x in inputs],
        out_specs=[VMEM] * len(outs),
        scratch_shapes=list(scratch),
        compiler_params=pltpu.CompilerParams(vmem_limit_bytes=16 << 20),
        cost_estimate=pl.CostEstimate(
            flops=int(micros * 1.15e9), bytes_accessed=1024, transcendentals=0
        ),
        name=name,
    )(*inputs)


def shape(*dims, dtype=f32):
    return jax.ShapeDtypeStruct(dims, dtype)


def nn(a, b):
    return jnp.dot(a, b, preferred_element_type=f32)


def nt(a, b):
    return lax.dot_general(a, b, (((1,), (1,)), ((), ())), preferred_element_type=f32)


def tn(a, b):
    return lax.dot_general(a, b, (((0,), (0,)), ((), ())), preferred_element_type=f32)


def embed_kernel(features_ref, weight_ref, labels_ref, pos_ref, loss_weight_ref, out_ref):
    n, width = features_ref.shape[0], weight_ref.shape[1]
    out_ref[:n, :] = nn(features_ref[...], weight_ref[...]).astype(bf16)
    out_ref[n:, :] = jnp.zeros((META, width), bf16)

    @pl.when(pl.program_id(0) == 0)
    def _():
        labels, pos, weight = labels_ref[...], pos_ref[...], loss_weight_ref[...]
        high = weight.astype(bf16).astype(f32)
        middle = (weight - high).astype(bf16).astype(f32)
        rows = [labels >> 7, labels & 127, pos // n, pos % n]
        rows = [x.astype(f32) for x in rows] + [high, middle, weight - high - middle]
        rows.append(jnp.zeros((META - 11, n), f32))
        out_ref[n:, :n] = jnp.concatenate(rows, axis=0).astype(bf16)


def embed(features, head_weight, labels, pos, loss_weight):
    n, depth = features.shape
    wide = head_weight.shape[1]
    step = wide // 2
    return pl.pallas_call(
        embed_kernel,
        grid=(wide // step,),
        out_shape=shape(n + META, wide, dtype=bf16),
        in_specs=[
            pl.BlockSpec((n, depth), lambda i: (0, 0)),
            pl.BlockSpec((depth, step), lambda i: (0, i)),
            pl.BlockSpec((1, n), lambda i: (0, 0)),
            pl.BlockSpec((3, n), lambda i: (0, 0)),
            pl.BlockSpec((1, n), lambda i: (0, 0)),
        ],
        out_specs=pl.BlockSpec((n + META, step), lambda i: (0, i)),
        compiler_params=pltpu.CompilerParams(vmem_limit_bytes=56 << 20),
        cost_estimate=pl.CostEstimate(flops=1 << 30, bytes_accessed=1 << 22, transcendentals=0),
        name="embed",
    )(features, head_weight, labels, pos, loss_weight)


def across(x, width):
    return jnp.concatenate([x] * (width // x.shape[1]), axis=1)


def score_block(
    rows_n, listed, tile, anchors_ref, labels_n, products_ref, coef_ref, lanes_ref, sq_ref,
    sums_ref,
):
    n = rows_n.shape[0]
    wide = rows_n.astype(f32)
    squares = jnp.sum(wide * wide, axis=1, keepdims=True) * BASE2
    sq_ref[...] = jnp.broadcast_to(jnp.where(listed, squares, MASKED), sq_ref.shape)
    lanes_ref[...] = jnp.zeros_like(lanes_ref)
    for i, part in enumerate(tile):
        lanes = slice(i * n, (i + 1) * n)
        products_ref[...] = nt(rows_n, part) * (2.0 * BASE2)
        base = [anchors_ref[k : k + 1, lanes] for k in range(3)]
        weight = anchors_ref[6:7, lanes]
        labels_a = anchors_ref[7:8, lanes]

        def step(c, carry, lanes=lanes, base=base, weight=weight, labels_a=labels_a):
            at = pl.multiple_of(c * CHUNK, CHUNK)
            rows = pl.ds(at, CHUNK)
            q = across(sq_ref[rows, :], n) - products_ref[rows, :]
            q = jnp.where(across(labels_n[rows, :], n) == labels_a, MASKED, q)
            y = [b - q for b in base]
            e = [jnp.exp2(-jnp.abs(v)) for v in y]
            a = [1.0 + v for v in e]
            a01 = a[0] * a[1]
            excess = e[0] + e[1] * a[0] + e[2] * a01
            total = 1.0 + excess
            inverse = 1.0 / total
            log_sum = jnp.log(total) + (excess - (total - 1.0))
            tops = jnp.maximum(y[0], 0.0) + jnp.maximum(y[1], 0.0) + jnp.maximum(y[2], 0.0)
            loss = tops * LN2 + log_sum
            inv2 = inverse * a[2]
            s = [inv2 * a[1], inv2 * a[0], inverse * a01]
            s = [v * jnp.where(w >= 0.0, 1.0, x) for v, w, x in zip(s, y, e)]
            coef = (s[0] + s[1] + s[2]) * weight
            coef_ref[rows, lanes] = coef.astype(bf16)
            folded = coef[:, :128]
            for j in range(128, n, 128):
                folded = folded + coef[:, j : j + 128]
            lanes_ref[rows, :] += folded
            fold = lambda v: jnp.sum(v.reshape(CHUNK // 8, 8, n), axis=0)
            return tuple(x + fold(v) for x, v in zip(carry, (*s, loss)))

        zero = jnp.zeros((8, n), f32)
        sums = lax.fori_loop(0, n // CHUNK, step, (zero,) * 4, unroll=4)
        for k, v in enumerate(sums):
            sums_ref[k : k + 1, lanes] += jnp.sum(v, axis=0, keepdims=True)


def negative_grad(rows_n, tile, coef_ref, lanes_ref):
    n = rows_n.shape[0]
    pulled = sum(nn(coef_ref[:, i * n : (i + 1) * n], part) for i, part in enumerate(tile))
    col_sums = jnp.sum(lanes_ref[...], axis=1, keepdims=True)
    return 2.0 * (pulled - col_sums * rows_n.astype(f32))


def column(row):
    n = row.shape[1]
    eye = lax.broadcasted_iota(jnp.int32, (n, n), 0) == lax.broadcasted_iota(jnp.int32, (n, n), 1)
    return jnp.sum(jnp.where(eye, jnp.broadcast_to(row, (n, n)), 0.0), axis=1, keepdims=True)


def meta_row(ref, n, i):
    return ref[n : n + META, :n].astype(f32)[i : i + 1, :]


def score_negatives(
    offset, scal_ref, p, tile, anchors_ref, coef_ref, sums_ref, grad_ref, products_ref, lanes_ref,
    sq_ref, label_ref,
):
    n = p.shape[0] - META
    labels = meta_row(p, n, 0) * 128.0 + meta_row(p, n, 1)
    label_ref[...] = jnp.broadcast_to(column(labels), label_ref.shape)
    rows_n = p[:n, :]
    score_block(
        rows_n, scal_ref[1 + offset] > 0, tile, anchors_ref, label_ref, products_ref, coef_ref,
        lanes_ref, sq_ref, sums_ref,
    )
    grad_ref[...] = negative_grad(rows_n, tile, coef_ref, lanes_ref).astype(grad_ref.dtype)


def own_kernel(
    scal_ref, p0, p1, p2, p3, n2, anchors_ref, c0, c2, sums_ref, grad0, grad2,
    products_ref, lanes_ref, sq_ref, label_ref,
):
    blocks = (p0, p1, p2, p3)
    n = p0.shape[0] - META
    me = scal_ref[0]
    scale = 1.0 / (3 * 4 * n)
    tile = [p[:n, :] for p in blocks]
    squares = []
    for part in tile:
        wide = part.astype(f32)
        squares.append(jnp.sum(wide * wide, axis=1, keepdims=True))
    for i, p in enumerate(blocks):
        lanes = slice(i * n, (i + 1) * n)
        meta = p[n : n + META, :n].astype(f32)
        where = []
        for k in range(3):
            holder = meta[2 + k : 3 + k, :].astype(jnp.int32) ^ me
            where.append(holder * n + meta[5 + k : 6 + k, :].astype(jnp.int32))
        found = [jnp.zeros((1, n), f32) for _ in range(3)]
        for j, part in enumerate(tile):
            apart = squares[j] - 2.0 * nt(part, tile[i])
            index = lax.broadcasted_iota(jnp.int32, (n, n), 0) + j * n
            for k in range(3):
                picked = jnp.where(index == where[k], apart, 0.0)
                found[k] = found[k] + jnp.sum(picked, axis=0, keepdims=True)
        for k in range(3):
            anchors_ref[k : k + 1, lanes] = (found[k] + SLACK_GAP) * BASE2
            anchors_ref[3 + k : 4 + k, lanes] = where[k].astype(f32)
        weight = meta[8:9, :] + meta[9:10, :] + meta[10:11, :]
        anchors_ref[6:7, lanes] = weight * scale
        anchors_ref[7:8, lanes] = meta[0:1, :] * 128.0 + meta[1:2, :]
    sums_ref[...] = jnp.zeros_like(sums_ref)
    for offset, p, coef_ref, grad_ref in ((0, p0, c0, grad0), (2, n2, c2, grad2)):
        score_negatives(
            offset, scal_ref, p, tile, anchors_ref, coef_ref, sums_ref, grad_ref, products_ref,
            lanes_ref, sq_ref, label_ref,
        )


def earlier_kernel(
    scal_ref, rows_ref, p0, p1, p2, p3, anchors_ref, before_ref, coef_ref, sums_ref,
    grad_ref, products_ref, lanes_ref, sq_ref, label_ref,
):
    n = p0.shape[0] - META
    tile = [p[:n, :] for p in (p0, p1, p2, p3)]
    sums_ref[...] = before_ref[...]
    score_negatives(
        1, scal_ref, rows_ref, tile, anchors_ref, coef_ref, sums_ref, grad_ref, products_ref,
        lanes_ref, sq_ref, label_ref,
    )
    for k in range(3):
        sums_ref[k : k + 1, :] = sums_ref[k : k + 1, :] * anchors_ref[6:7, :]


def anchor_kernel(first, c0, c1, c2, n0, n1, n2, keep_ref, send_ref):
    n = n0.shape[0] - META
    for i, ref in ((first, keep_ref), (first + 1, send_ref)):
        lanes = slice(i * n, (i + 1) * n)
        total = tn(c0[:, lanes], n0[:n, :])
        total = total + tn(c1[:, lanes], n1[:n, :]) + tn(c2[:, lanes], n2[:n, :])
        ref[...] = 2.0 * total


def halved_kernel(keep_ref, other_ref, out_ref):
    out_ref[...] = (keep_ref[...] + other_ref[...]).astype(bf16)


def listed_kernel(
    anchors_ref, s0, s1, s2, s3, p0, p1, p2, p3, keep_ref, other_ref, own_ref, out_ref, loss_ref
):
    n = p0.shape[0] - META
    tile = [p[:n, :] for p in (p0, p1, p2, p3)]
    sums = []
    for i in range(4):
        parts = [s[:, (i ^ j) * n : ((i ^ j) + 1) * n] for j, s in enumerate((s0, s1, s2, s3))]
        sums.append((parts[0] + parts[1]) + (parts[2] + parts[3]))
    loss_ref[...] = sums[0][3:4, :] * (1.0 / (SMOOTHING_SCALE * 3 * 4 * n))
    own_coef = [column(sums[0][k : k + 1, :]) for k in range(3)]
    own_where = [column(anchors_ref[3 + k : 4 + k, :n]) for k in range(3)]
    total = jnp.zeros(out_ref.shape, f32)
    pushed = jnp.zeros((n, 1), f32)
    for i, part in enumerate(tile):
        lanes = slice(i * n, (i + 1) * n)
        mine = lax.broadcasted_iota(jnp.int32, (n, n), 0).astype(f32)
        others = (lax.broadcasted_iota(jnp.int32, (n, n), 1) + i * n).astype(f32)
        matrix = jnp.zeros((n, n), f32)
        for k in range(3):
            hit = anchors_ref[3 + k : 4 + k, lanes] == mine
            matrix = matrix + jnp.where(hit, sums[i][k : k + 1, :], 0.0)
        pushed = pushed + jnp.sum(matrix, axis=1, keepdims=True)
        for k in range(3):
            matrix = matrix + jnp.where(own_where[k] == others, own_coef[k], 0.0)
        high = matrix.astype(bf16)
        low = (matrix - high.astype(f32)).astype(bf16)
        total = total + nn(high, part) + nn(low, part)
    base = keep_ref[...] + other_ref[...] + own_ref[...]
    out_ref[...] = base + 2.0 * (pushed * tile[0].astype(f32) - total)


def passed_kernel(scal_ref, grad_ref, swapped_ref, out_ref):
    extra = jnp.where(scal_ref[4] > 0, swapped_ref[...].astype(f32), 0.0)
    out_ref[...] = (grad_ref[...] + extra).astype(bf16)


def gathered_kernel(scal_ref, base_ref, y_ref, swapped_ref, two_ref, out_ref):
    extra = jnp.where(scal_ref[4] > 0, 0.0, swapped_ref[...].astype(f32))
    total = base_ref[...] + y_ref[...].astype(f32)
    out_ref[...] = (total + (extra + two_ref[...].astype(f32))).astype(bf16)


def chosen_kernel(scal_ref, own_ref, other_ref, out_ref):
    out_ref[...] = jnp.where(scal_ref[4] > 0, other_ref[...], own_ref[...])


def head_kernel(f0, f1, f2, f3, g0, g1, g2, g3, out_ref):
    total = nn(f0[...], g0[...]) + nn(f1[...], g1[...])
    total = total + nn(f2[...], g2[...]) + nn(f3[...], g3[...])
    out_ref[...] = total.astype(bf16)


def local(features, head_weight, labels, pos_index, pair_mask, loss_weight):
    blks, rows_n = lax.axis_size("blk"), lax.axis_size("rows")
    me = lax.axis_index("rows")
    n, depth = features.shape
    wide = head_weight.shape[1]
    slice_rows = depth // (blks * rows_n)

    def over_rows(x, flip):
        return lax.ppermute(x, "rows", [(i, i ^ flip) for i in range(rows_n)])

    def two_on(x, by):
        return lax.ppermute(x, "blk", [(b, (b + by) % blks) for b in range(blks)])

    def swapped(x):
        pairs = [
            (b * rows_n + i, (b ^ 1) * rows_n + (i ^ 2)) for b in range(blks) for i in range(rows_n)
        ]
        return lax.ppermute(x, ("blk", "rows"), pairs)

    odd = lax.axis_index("blk") % 2
    scal = jnp.concatenate([me[None], pair_mask[0], odd[None]]).astype(jnp.int32)
    p0 = embed(features, head_weight, labels[None], pos_index.T, loss_weight[None])
    p2 = over_rows(p0, 2)
    n2 = two_on(p0, 2)
    p1 = over_rows(p0, 1)

    features, _ = lax.optimization_barrier((features, p0))
    m = blks * slice_rows
    turned = features.T.reshape(blks, rows_n, slice_rows, n)
    turned = [
        lax.dynamic_index_in_dim(turned, me ^ j, 1, keepdims=False).reshape(m, n) for j in range(4)
    ]
    f0 = turned[0]
    p2, *turned = lax.optimization_barrier((p2, *turned))
    p3 = over_rows(p2, 1)
    f1 = over_rows(turned[1], 1)
    f2, f3 = over_rows(turned[2], 2), over_rows(turned[3], 2)

    (chosen,) = call(
        chosen_kernel,
        (scal, p0, n2),
        [shape(n + META, wide, dtype=bf16)],
        micros=0.01,
        name="row_choice",
    )
    n1 = swapped(chosen)
    scratch = [pltpu.VMEM((n, n), f32)] + [pltpu.VMEM((n, 128), f32)] * 3
    tile = (p0, p1, p2, p3)
    low_grad = shape(n, wide, dtype=bf16)
    low_coef = shape(n, 4 * n, dtype=bf16)
    anchors, c0, c2, sums, own_grad, grad2 = call(
        own_kernel,
        (scal, *tile, n2),
        [shape(8, 4 * n), low_coef, low_coef, shape(8, 4 * n), shape(n, wide), shape(n, wide)],
        scratch,
        micros=0.01,
        name="own_and_two_before",
    )
    c1, s0, grad1 = call(
        earlier_kernel,
        (scal, n1, *tile, anchors, sums),
        [low_coef, shape(8, 4 * n), low_grad],
        scratch,
        micros=0.01,
        name="block_before",
    )
    grad1 = swapped(grad1)
    c1, f2, f3 = lax.optimization_barrier((c1, f2, f3))
    s2 = over_rows(s0, 2)
    s1 = over_rows(s0, 1)
    pieces = (c0, c1, c2, p0, n1, n2)
    rows_f32 = [shape(n, wide), shape(n, wide)]
    keep, send = call(
        functools.partial(anchor_kernel, 2), pieces, rows_f32, micros=0.01, name="anchor_grad_across"
    )
    keep, f1, s2 = lax.optimization_barrier((keep, f1, s2))
    (half,) = call(
        halved_kernel, (keep, over_rows(send, 1)), [low_grad], micros=0.01, name="half_sum"
    )
    from_y = over_rows(half, 2)
    grad2, _ = lax.optimization_barrier((grad2, half))
    (grad2,) = call(
        passed_kernel, (scal, grad2, grad1), [low_grad], micros=0.01, name="passed_grad"
    )
    grad2 = two_on(grad2, -2)
    f3, s3 = over_rows(f3, 1), over_rows(s2, 1)
    keep, send = call(
        functools.partial(anchor_kernel, 0), pieces, rows_f32, micros=0.01, name="anchor_grad_own"
    )
    s1, s3, f3 = lax.optimization_barrier((s1, s3, f3))
    base, anchor_loss = call(
        listed_kernel,
        (anchors, s0, s1, s2, s3, *tile, keep, over_rows(send, 1), own_grad),
        [shape(n, wide), shape(1, n)],
        micros=0.01,
        name="listed",
    )
    (g0,) = call(
        gathered_kernel, (scal, base, from_y, grad1, grad2), [low_grad], micros=0.01, name="row_grad"
    )
    g2 = over_rows(g0, 2)
    g1 = over_rows(g0, 1)
    g3 = over_rows(g2, 1)
    (part,) = call(
        head_kernel,
        (f0, f1, f2, f3, g0, g1, g2, g3),
        [shape(m, wide, dtype=bf16)],
        micros=0.01, name="head_grad",
    )
    parts = lax.all_to_all(part, "blk", split_axis=0, concat_axis=0, tiled=True)
    weight_grad = jnp.sum(parts.reshape(blks, slice_rows, wide).astype(f32), axis=0)
    return anchor_loss[0], weight_grad


def solution(mesh):
    return jax.shard_map(
        local,
        mesh=mesh,
        in_specs=(
            P(("blk", "rows"), None),
            P(),
            P(("blk", "rows")),
            P(("blk", "rows"), None),
            P("blk", None),
            P(("blk", "rows")),
        ),
        out_specs=(P(("blk", "rows")), P(("blk", "rows"), None)),
        check_vma=False,
    )
```

```python
import functools

import jax
import jax.numpy as jnp
from jax import lax
from jax.experimental import pallas as pl
from jax.experimental.pallas import tpu as pltpu
from jax.sharding import PartitionSpec as P

SMOOTHING_SCALE = 16.0
SLACK_GAP = 0.1
LN2 = 0.6931471805599453
BASE2 = SMOOTHING_SCALE / LN2
MASKED = 1e30
META = 16
CHUNK = 16
f32 = jnp.float32
bf16 = jnp.bfloat16

VMEM = pl.BlockSpec(memory_space=pltpu.VMEM)
SMEM = pl.BlockSpec(memory_space=pltpu.SMEM)


def call(kernel, inputs, outs, scratch=(), name=None):
    return pl.pallas_call(
        kernel,
        out_shape=outs,
        in_specs=[SMEM if x.ndim == 1 else VMEM for x in inputs],
        out_specs=[VMEM] * len(outs),
        scratch_shapes=list(scratch),
        compiler_params=pltpu.CompilerParams(vmem_limit_bytes=16 << 20),
        cost_estimate=pl.CostEstimate(
            flops=1 << 20, bytes_accessed=1024, transcendentals=0
        ),
        name=name,
    )(*inputs)


def shape(*dims, dtype=f32):
    return jax.ShapeDtypeStruct(dims, dtype)


def nn(a, b):
    return jnp.dot(a, b, preferred_element_type=f32)


def nt(a, b):
    return lax.dot_general(a, b, (((1,), (1,)), ((), ())), preferred_element_type=f32)


def tn(a, b):
    return lax.dot_general(a, b, (((0,), (0,)), ((), ())), preferred_element_type=f32)


def embed_kernel(features_ref, weight_ref, labels_ref, pos_ref, loss_weight_ref, out_ref):
    n, width = features_ref.shape[0], weight_ref.shape[1]
    out_ref[:n, :] = nn(features_ref[...], weight_ref[...]).astype(bf16)
    out_ref[n:, :] = jnp.zeros((META, width), bf16)

    @pl.when(pl.program_id(0) == 0)
    def _():
        labels, pos, weight = labels_ref[...], pos_ref[...], loss_weight_ref[...]
        high = weight.astype(bf16).astype(f32)
        middle = (weight - high).astype(bf16).astype(f32)
        rows = [labels >> 7, labels & 127, pos // n, pos % n]
        rows = [x.astype(f32) for x in rows] + [high, middle, weight - high - middle]
        rows.append(jnp.zeros((META - 11, n), f32))
        out_ref[n:, :n] = jnp.concatenate(rows, axis=0).astype(bf16)


def embed(features, head_weight, labels, pos, loss_weight):
    n, depth = features.shape
    wide = head_weight.shape[1]
    step = wide // 2
    return pl.pallas_call(
        embed_kernel,
        grid=(wide // step,),
        out_shape=shape(n + META, wide, dtype=bf16),
        in_specs=[
            pl.BlockSpec((n, depth), lambda i: (0, 0)),
            pl.BlockSpec((depth, step), lambda i: (0, i)),
            pl.BlockSpec((1, n), lambda i: (0, 0)),
            pl.BlockSpec((3, n), lambda i: (0, 0)),
            pl.BlockSpec((1, n), lambda i: (0, 0)),
        ],
        out_specs=pl.BlockSpec((n + META, step), lambda i: (0, i)),
        compiler_params=pltpu.CompilerParams(vmem_limit_bytes=56 << 20),
        cost_estimate=pl.CostEstimate(flops=1 << 30, bytes_accessed=1 << 22, transcendentals=0),
        name="embed",
    )(features, head_weight, labels, pos, loss_weight)


def across(x, width):
    return jnp.concatenate([x] * (width // x.shape[1]), axis=1)


def score_block(
    rows_n, listed, tile, anchors_ref, labels_n, products_ref, coef_ref, lanes_ref, sq_ref,
    sums_ref,
):
    n = rows_n.shape[0]
    wide = rows_n.astype(f32)
    squares = jnp.sum(wide * wide, axis=1, keepdims=True) * BASE2
    sq_ref[...] = jnp.broadcast_to(jnp.where(listed, squares, MASKED), sq_ref.shape)
    lanes_ref[...] = jnp.zeros_like(lanes_ref)
    for i, part in enumerate(tile):
        lanes = slice(i * n, (i + 1) * n)
        products_ref[...] = nt(rows_n, part) * (2.0 * BASE2)
        base = [anchors_ref[k : k + 1, lanes] for k in range(3)]
        weight = anchors_ref[6:7, lanes]
        labels_a = anchors_ref[7:8, lanes]

        def step(c, carry, lanes=lanes, base=base, weight=weight, labels_a=labels_a):
            at = pl.multiple_of(c * CHUNK, CHUNK)
            rows = pl.ds(at, CHUNK)
            q = across(sq_ref[rows, :], n) - products_ref[rows, :]
            q = jnp.where(across(labels_n[rows, :], n) == labels_a, MASKED, q)
            y = [b - q for b in base]
            e = [jnp.exp2(-jnp.abs(v)) for v in y]
            a = [1.0 + v for v in e]
            a01 = a[0] * a[1]
            excess = e[0] + e[1] * a[0] + e[2] * a01
            total = 1.0 + excess
            inverse = 1.0 / total
            log_sum = jnp.log(total) + (excess - (total - 1.0))
            tops = jnp.maximum(y[0], 0.0) + jnp.maximum(y[1], 0.0) + jnp.maximum(y[2], 0.0)
            loss = tops * LN2 + log_sum
            inv2 = inverse * a[2]
            s = [inv2 * a[1], inv2 * a[0], inverse * a01]
            s = [v * jnp.where(w >= 0.0, 1.0, x) for v, w, x in zip(s, y, e)]
            coef = (s[0] + s[1] + s[2]) * weight
            coef_ref[rows, lanes] = coef.astype(bf16)
            folded = coef[:, :128]
            for j in range(128, n, 128):
                folded = folded + coef[:, j : j + 128]
            lanes_ref[rows, :] += folded
            fold = lambda v: jnp.sum(v.reshape(CHUNK // 8, 8, n), axis=0)
            return tuple(x + fold(v) for x, v in zip(carry, (*s, loss)))

        zero = jnp.zeros((8, n), f32)
        sums = lax.fori_loop(0, n // CHUNK, step, (zero,) * 4, unroll=4)
        for k, v in enumerate(sums):
            sums_ref[k : k + 1, lanes] += jnp.sum(v, axis=0, keepdims=True)


def negative_grad(rows_n, tile, coef_ref, lanes_ref):
    n = rows_n.shape[0]
    pulled = sum(nn(coef_ref[:, i * n : (i + 1) * n], part) for i, part in enumerate(tile))
    col_sums = jnp.sum(lanes_ref[...], axis=1, keepdims=True)
    return 2.0 * (pulled - col_sums * rows_n.astype(f32))


def column(row):
    n = row.shape[1]
    eye = lax.broadcasted_iota(jnp.int32, (n, n), 0) == lax.broadcasted_iota(jnp.int32, (n, n), 1)
    return jnp.sum(jnp.where(eye, jnp.broadcast_to(row, (n, n)), 0.0), axis=1, keepdims=True)


def meta_row(ref, n, i):
    return ref[n : n + META, :n].astype(f32)[i : i + 1, :]


def score_negatives(
    offset, scal_ref, p, tile, anchors_ref, coef_ref, sums_ref, grad_ref, products_ref, lanes_ref,
    sq_ref, label_ref,
):
    n = p.shape[0] - META
    labels = meta_row(p, n, 0) * 128.0 + meta_row(p, n, 1)
    label_ref[...] = jnp.broadcast_to(column(labels), label_ref.shape)
    rows_n = p[:n, :]
    score_block(
        rows_n, scal_ref[1 + offset] > 0, tile, anchors_ref, label_ref, products_ref, coef_ref,
        lanes_ref, sq_ref, sums_ref,
    )
    grad_ref[...] = negative_grad(rows_n, tile, coef_ref, lanes_ref).astype(grad_ref.dtype)


def own_kernel(
    scal_ref, p0, p1, p2, p3, n2, anchors_ref, c0, c2, sums_ref, grad0, grad2,
    products_ref, lanes_ref, sq_ref, label_ref,
):
    blocks = (p0, p1, p2, p3)
    n = p0.shape[0] - META
    me = scal_ref[0]
    scale = 1.0 / (3 * 4 * n)
    tile = [p[:n, :] for p in blocks]
    squares = []
    for part in tile:
        wide = part.astype(f32)
        squares.append(jnp.sum(wide * wide, axis=1, keepdims=True))
    for i, p in enumerate(blocks):
        lanes = slice(i * n, (i + 1) * n)
        meta = p[n : n + META, :n].astype(f32)
        where = []
        for k in range(3):
            holder = meta[2 + k : 3 + k, :].astype(jnp.int32) ^ me
            where.append(holder * n + meta[5 + k : 6 + k, :].astype(jnp.int32))
        found = [jnp.zeros((1, n), f32) for _ in range(3)]
        for j, part in enumerate(tile):
            apart = squares[j] - 2.0 * nt(part, tile[i])
            index = lax.broadcasted_iota(jnp.int32, (n, n), 0) + j * n
            for k in range(3):
                picked = jnp.where(index == where[k], apart, 0.0)
                found[k] = found[k] + jnp.sum(picked, axis=0, keepdims=True)
        for k in range(3):
            anchors_ref[k : k + 1, lanes] = (found[k] + SLACK_GAP) * BASE2
            anchors_ref[3 + k : 4 + k, lanes] = where[k].astype(f32)
        weight = meta[8:9, :] + meta[9:10, :] + meta[10:11, :]
        anchors_ref[6:7, lanes] = weight * scale
        anchors_ref[7:8, lanes] = meta[0:1, :] * 128.0 + meta[1:2, :]
    sums_ref[...] = jnp.zeros_like(sums_ref)
    for offset, p, coef_ref, grad_ref in ((0, p0, c0, grad0), (2, n2, c2, grad2)):
        score_negatives(
            offset, scal_ref, p, tile, anchors_ref, coef_ref, sums_ref, grad_ref, products_ref,
            lanes_ref, sq_ref, label_ref,
        )


def last_kernel(
    scal_ref, n1, n2, p0, p1, p2, p3, c0, c2, anchors_ref, before_ref, sums_ref, grad_ref,
    keep0, send1, keep2, send3, coef_ref, products_ref, lanes_ref, sq_ref, label_ref,
):
    n = p0.shape[0] - META
    tile = [p[:n, :] for p in (p0, p1, p2, p3)]
    sums_ref[...] = before_ref[...]
    score_negatives(
        1, scal_ref, n1, tile, anchors_ref, coef_ref, sums_ref, grad_ref, products_ref,
        lanes_ref, sq_ref, label_ref,
    )
    for k in range(3):
        sums_ref[k : k + 1, :] = sums_ref[k : k + 1, :] * anchors_ref[6:7, :]
    for i, ref in enumerate((keep0, send1, keep2, send3)):
        lanes = slice(i * n, (i + 1) * n)
        total = tn(c0[:, lanes], p0[:n, :])
        total = total + tn(coef_ref[:, lanes], n1[:n, :]) + tn(c2[:, lanes], n2[:n, :])
        ref[...] = 2.0 * total


def halved_kernel(keep_ref, other_ref, out_ref):
    out_ref[...] = (keep_ref[...] + other_ref[...]).astype(bf16)


def listed_kernel(
    anchors_ref, s0, s1, s2, s3, p0, p1, p2, p3, keep_ref, other_ref, own_ref, out_ref, loss_ref
):
    n = p0.shape[0] - META
    tile = [p[:n, :] for p in (p0, p1, p2, p3)]
    sums = []
    for i in range(4):
        parts = [s[:, (i ^ j) * n : ((i ^ j) + 1) * n] for j, s in enumerate((s0, s1, s2, s3))]
        sums.append((parts[0] + parts[1]) + (parts[2] + parts[3]))
    loss_ref[...] = sums[0][3:4, :] * (1.0 / (SMOOTHING_SCALE * 3 * 4 * n))
    own_coef = [column(sums[0][k : k + 1, :]) for k in range(3)]
    own_where = [column(anchors_ref[3 + k : 4 + k, :n]) for k in range(3)]
    total = jnp.zeros(out_ref.shape, f32)
    pushed = jnp.zeros((n, 1), f32)
    for i, part in enumerate(tile):
        lanes = slice(i * n, (i + 1) * n)
        mine = lax.broadcasted_iota(jnp.int32, (n, n), 0).astype(f32)
        others = (lax.broadcasted_iota(jnp.int32, (n, n), 1) + i * n).astype(f32)
        matrix = jnp.zeros((n, n), f32)
        for k in range(3):
            hit = anchors_ref[3 + k : 4 + k, lanes] == mine
            matrix = matrix + jnp.where(hit, sums[i][k : k + 1, :], 0.0)
        pushed = pushed + jnp.sum(matrix, axis=1, keepdims=True)
        for k in range(3):
            matrix = matrix + jnp.where(own_where[k] == others, own_coef[k], 0.0)
        high = matrix.astype(bf16)
        low = (matrix - high.astype(f32)).astype(bf16)
        total = total + nn(high, part) + nn(low, part)
    base = keep_ref[...] + other_ref[...] + own_ref[...]
    out_ref[...] = base + 2.0 * (pushed * tile[0].astype(f32) - total)


def gathered_kernel(base_ref, y_ref, one_ref, two_ref, out_ref):
    total = base_ref[...] + y_ref[...].astype(f32)
    out_ref[...] = (total + (one_ref[...].astype(f32) + two_ref[...].astype(f32))).astype(bf16)


def chosen_kernel(scal_ref, own_ref, other_ref, out_ref):
    out_ref[...] = jnp.where(scal_ref[4] > 0, other_ref[...], own_ref[...])


def head_kernel(f0, f1, f2, f3, g0, g1, g2, g3, out_ref):
    total = nn(f0[...], g0[...]) + nn(f1[...], g1[...])
    total = total + nn(f2[...], g2[...]) + nn(f3[...], g3[...])
    out_ref[...] = total.astype(bf16)


def local(features, head_weight, labels, pos_index, pair_mask, loss_weight):
    blks, rows_n = lax.axis_size("blk"), lax.axis_size("rows")
    me = lax.axis_index("rows")
    n, depth = features.shape
    wide = head_weight.shape[1]
    slice_rows = depth // (blks * rows_n)

    def over_rows(x, flip):
        return lax.ppermute(x, "rows", [(i, i ^ flip) for i in range(rows_n)])

    def two_on(x, by):
        return lax.ppermute(x, "blk", [(b, (b + by) % blks) for b in range(blks)])

    def swapped(x):
        pairs = [
            (b * rows_n + i, (b ^ 1) * rows_n + (i ^ 2)) for b in range(blks) for i in range(rows_n)
        ]
        return lax.ppermute(x, ("blk", "rows"), pairs)

    def one_back(x):
        pairs = [
            (b * rows_n + i, (b - 1) % blks * rows_n + (i ^ 2))
            for b in range(blks)
            for i in range(rows_n)
        ]
        return lax.ppermute(x, ("blk", "rows"), pairs)

    odd = lax.axis_index("blk") % 2
    scal = jnp.concatenate([me[None], pair_mask[0], odd[None]]).astype(jnp.int32)
    p0 = embed(features, head_weight, labels[None], pos_index.T, loss_weight[None])
    p2 = over_rows(p0, 2)
    n2 = two_on(p0, 2)
    p1 = over_rows(p0, 1)

    features, _ = lax.optimization_barrier((features, p0))
    m = blks * slice_rows
    turned = features.T.reshape(blks, rows_n, slice_rows, n)
    turned = [
        lax.dynamic_index_in_dim(turned, me ^ j, 1, keepdims=False).reshape(m, n) for j in range(4)
    ]
    f0 = turned[0]
    p2, *turned = lax.optimization_barrier((p2, *turned))
    p3 = over_rows(p2, 1)
    f1 = over_rows(turned[1], 1)
    f2, f3 = over_rows(turned[2], 2), over_rows(turned[3], 2)

    (chosen,) = call(
        chosen_kernel,
        (scal, p0, n2),
        [shape(n + META, wide, dtype=bf16)],
        name="row_choice",
    )
    n1 = swapped(chosen)
    scratch = [pltpu.VMEM((n, n), f32)] + [pltpu.VMEM((n, 128), f32)] * 3
    tile = (p0, p1, p2, p3)
    low_grad = shape(n, wide, dtype=bf16)
    low_coef = shape(n, 4 * n, dtype=bf16)
    anchors, c0, c2, sums, own_grad, grad2 = call(
        own_kernel,
        (scal, *tile, n2),
        [shape(8, 4 * n), low_coef, low_coef, shape(8, 4 * n), shape(n, wide), low_grad],
        scratch,
        name="own_and_two_before",
    )
    grad2 = two_on(grad2, -2)
    s0, grad1, keep0, send1, keep2, send3 = call(
        last_kernel,
        (scal, n1, n2, *tile, c0, c2, anchors, sums),
        [shape(8, 4 * n), low_grad] + [shape(n, wide)] * 4,
        [pltpu.VMEM((n, 4 * n), bf16), *scratch],
        name="block_before",
    )
    grad1 = one_back(grad1)
    s2 = over_rows(s0, 2)
    s1 = over_rows(s0, 1)
    send3, grad2, f2, f3 = lax.optimization_barrier((send3, grad2, f2, f3))
    other3 = over_rows(send3, 1)
    keep2, f1, f2, f3, s2 = lax.optimization_barrier((keep2, f1, f2, f3, s2))
    (half,) = call(halved_kernel, (keep2, other3), [low_grad], name="half_sum")
    from_y = over_rows(half, 2)
    f3, s3 = over_rows(f3, 1), over_rows(s2, 1)
    s1, s3, f3 = lax.optimization_barrier((s1, s3, f3))
    base, anchor_loss = call(
        listed_kernel,
        (anchors, s0, s1, s2, s3, *tile, keep0, over_rows(send1, 1), own_grad),
        [shape(n, wide), shape(1, n)],
        name="listed",
    )
    (g0,) = call(
        gathered_kernel, (base, from_y, grad1, grad2), [low_grad], name="row_grad"
    )
    g2 = over_rows(g0, 2)
    g1 = over_rows(g0, 1)
    g3 = over_rows(g2, 1)
    (part,) = call(
        head_kernel,
        (f0, f1, f2, f3, g0, g1, g2, g3),
        [shape(m, wide, dtype=bf16)],
        name="head_grad",
    )
    parts = lax.all_to_all(part, "blk", split_axis=0, concat_axis=0, tiled=True)
    weight_grad = jnp.sum(parts.reshape(blks, slice_rows, wide).astype(f32), axis=0)
    return anchor_loss[0], weight_grad


def solution(mesh):
    return jax.shard_map(
        local,
        mesh=mesh,
        in_specs=(
            P(("blk", "rows"), None),
            P(),
            P(("blk", "rows")),
            P(("blk", "rows"), None),
            P("blk", None),
            P(("blk", "rows")),
        ),
        out_specs=(P(("blk", "rows")), P(("blk", "rows"), None)),
        check_vma=False,
    )
```

```python
import functools

import jax
import jax.numpy as jnp
from jax import lax
from jax.experimental import pallas as pl
from jax.experimental.pallas import tpu as pltpu
from jax.sharding import PartitionSpec as P

SMOOTHING_SCALE = 16.0
SLACK_GAP = 0.1
LN2 = 0.6931471805599453
BASE2 = SMOOTHING_SCALE / LN2
MASKED = 1e30
META = 16
CHUNK = 16
f32 = jnp.float32
bf16 = jnp.bfloat16

VMEM = pl.BlockSpec(memory_space=pltpu.VMEM)
SMEM = pl.BlockSpec(memory_space=pltpu.SMEM)


def call(kernel, inputs, outs, scratch=(), name=None):
    return pl.pallas_call(
        kernel,
        out_shape=outs,
        in_specs=[SMEM if x.ndim == 1 else VMEM for x in inputs],
        out_specs=[VMEM] * len(outs),
        scratch_shapes=list(scratch),
        compiler_params=pltpu.CompilerParams(vmem_limit_bytes=16 << 20),
        cost_estimate=pl.CostEstimate(
            flops=1 << 20, bytes_accessed=1024, transcendentals=0
        ),
        name=name,
    )(*inputs)


def shape(*dims, dtype=f32):
    return jax.ShapeDtypeStruct(dims, dtype)


def nn(a, b):
    return jnp.dot(a, b, preferred_element_type=f32)


def nt(a, b):
    return lax.dot_general(a, b, (((1,), (1,)), ((), ())), preferred_element_type=f32)


def tn(a, b):
    return lax.dot_general(a, b, (((0,), (0,)), ((), ())), preferred_element_type=f32)


def embed_kernel(features_ref, weight_ref, labels_ref, pos_ref, loss_weight_ref, out_ref):
    n, width = features_ref.shape[0], weight_ref.shape[1]
    out_ref[:n, :] = nn(features_ref[...], weight_ref[...]).astype(bf16)
    out_ref[n:, :] = jnp.zeros((META, width), bf16)

    @pl.when(pl.program_id(0) == 0)
    def _():
        labels, pos, weight = labels_ref[...], pos_ref[...], loss_weight_ref[...]
        high = weight.astype(bf16).astype(f32)
        middle = (weight - high).astype(bf16).astype(f32)
        rows = [labels >> 7, labels & 127, pos // n, pos % n]
        rows = [x.astype(f32) for x in rows] + [high, middle, weight - high - middle]
        rows.append(jnp.zeros((META - 11, n), f32))
        out_ref[n:, :n] = jnp.concatenate(rows, axis=0).astype(bf16)


def embed(features, head_weight, labels, pos, loss_weight):
    n, depth = features.shape
    wide = head_weight.shape[1]
    step = wide // 2
    return pl.pallas_call(
        embed_kernel,
        grid=(wide // step,),
        out_shape=shape(n + META, wide, dtype=bf16),
        in_specs=[
            pl.BlockSpec((n, depth), lambda i: (0, 0)),
            pl.BlockSpec((depth, step), lambda i: (0, i)),
            pl.BlockSpec((1, n), lambda i: (0, 0)),
            pl.BlockSpec((3, n), lambda i: (0, 0)),
            pl.BlockSpec((1, n), lambda i: (0, 0)),
        ],
        out_specs=pl.BlockSpec((n + META, step), lambda i: (0, i)),
        compiler_params=pltpu.CompilerParams(vmem_limit_bytes=56 << 20),
        cost_estimate=pl.CostEstimate(flops=1 << 30, bytes_accessed=1 << 22, transcendentals=0),
        name="embed",
    )(features, head_weight, labels, pos, loss_weight)


def across(x, width):
    return jnp.concatenate([x] * (width // x.shape[1]), axis=1)


def score_block(
    rows_n, listed, tile, anchors_ref, labels_n, products_ref, coef_ref, lanes_ref, sq_ref,
    sums_ref,
):
    n = rows_n.shape[0]
    wide = rows_n.astype(f32)
    squares = jnp.sum(wide * wide, axis=1, keepdims=True) * BASE2
    sq_ref[...] = jnp.broadcast_to(jnp.where(listed, squares, MASKED), sq_ref.shape)
    lanes_ref[...] = jnp.zeros_like(lanes_ref)
    for i, part in enumerate(tile):
        lanes = slice(i * n, (i + 1) * n)
        products_ref[...] = nt(rows_n, part) * (2.0 * BASE2)
        base = [anchors_ref[k : k + 1, lanes] for k in range(3)]
        weight = anchors_ref[6:7, lanes]
        labels_a = anchors_ref[7:8, lanes]

        def step(c, carry, lanes=lanes, base=base, weight=weight, labels_a=labels_a):
            at = pl.multiple_of(c * CHUNK, CHUNK)
            rows = pl.ds(at, CHUNK)
            q = across(sq_ref[rows, :], n) - products_ref[rows, :]
            q = jnp.where(across(labels_n[rows, :], n) == labels_a, MASKED, q)
            y = [b - q for b in base]
            e = [jnp.exp2(-jnp.abs(v)) for v in y]
            a = [1.0 + v for v in e]
            a01 = a[0] * a[1]
            excess = e[0] + e[1] * a[0] + e[2] * a01
            total = 1.0 + excess
            inverse = 1.0 / total
            log_sum = jnp.log(total) + (excess - (total - 1.0))
            tops = jnp.maximum(y[0], 0.0) + jnp.maximum(y[1], 0.0) + jnp.maximum(y[2], 0.0)
            loss = tops * LN2 + log_sum
            inv2 = inverse * a[2]
            s = [inv2 * a[1], inv2 * a[0], inverse * a01]
            s = [v * jnp.where(w >= 0.0, 1.0, x) for v, w, x in zip(s, y, e)]
            coef = (s[0] + s[1] + s[2]) * weight
            coef_ref[rows, lanes] = coef.astype(bf16)
            folded = coef[:, :128]
            for j in range(128, n, 128):
                folded = folded + coef[:, j : j + 128]
            lanes_ref[rows, :] += folded
            fold = lambda v: jnp.sum(v.reshape(CHUNK // 8, 8, n), axis=0)
            return tuple(x + fold(v) for x, v in zip(carry, (*s, loss)))

        zero = jnp.zeros((8, n), f32)
        sums = lax.fori_loop(0, n // CHUNK, step, (zero,) * 4, unroll=4)
        for k, v in enumerate(sums):
            sums_ref[k : k + 1, lanes] += jnp.sum(v, axis=0, keepdims=True)


def negative_grad(rows_n, tile, coef_ref, lanes_ref):
    n = rows_n.shape[0]
    pulled = sum(nn(coef_ref[:, i * n : (i + 1) * n], part) for i, part in enumerate(tile))
    col_sums = jnp.sum(lanes_ref[...], axis=1, keepdims=True)
    return 2.0 * (pulled - col_sums * rows_n.astype(f32))


def column(row):
    n = row.shape[1]
    eye = lax.broadcasted_iota(jnp.int32, (n, n), 0) == lax.broadcasted_iota(jnp.int32, (n, n), 1)
    return jnp.sum(jnp.where(eye, jnp.broadcast_to(row, (n, n)), 0.0), axis=1, keepdims=True)


def meta_row(ref, n, i):
    return ref[n : n + META, :n].astype(f32)[i : i + 1, :]


def score_negatives(
    offset, scal_ref, p, tile, anchors_ref, coef_ref, sums_ref, grad_ref, products_ref, lanes_ref,
    sq_ref, label_ref,
):
    n = p.shape[0] - META
    labels = meta_row(p, n, 0) * 128.0 + meta_row(p, n, 1)
    label_ref[...] = jnp.broadcast_to(column(labels), label_ref.shape)
    rows_n = p[:n, :]
    score_block(
        rows_n, scal_ref[1 + offset] > 0, tile, anchors_ref, label_ref, products_ref, coef_ref,
        lanes_ref, sq_ref, sums_ref,
    )
    grad_ref[...] = negative_grad(rows_n, tile, coef_ref, lanes_ref).astype(grad_ref.dtype)


def own_kernel(
    scal_ref, p0, p1, p2, p3, n2, anchors_ref, c0, c2, sums_ref, grad0, grad2,
    products_ref, lanes_ref, sq_ref, label_ref,
):
    blocks = (p0, p1, p2, p3)
    n = p0.shape[0] - META
    me = scal_ref[0]
    scale = 1.0 / (3 * 4 * n)
    tile = [p[:n, :] for p in blocks]
    squares = []
    for part in tile:
        wide = part.astype(f32)
        squares.append(jnp.sum(wide * wide, axis=1, keepdims=True))
    for i, p in enumerate(blocks):
        lanes = slice(i * n, (i + 1) * n)
        meta = p[n : n + META, :n].astype(f32)
        where = []
        for k in range(3):
            holder = meta[2 + k : 3 + k, :].astype(jnp.int32) ^ me
            where.append(holder * n + meta[5 + k : 6 + k, :].astype(jnp.int32))
        found = [jnp.zeros((1, n), f32) for _ in range(3)]
        for j, part in enumerate(tile):
            apart = squares[j] - 2.0 * nt(part, tile[i])
            index = lax.broadcasted_iota(jnp.int32, (n, n), 0) + j * n
            for k in range(3):
                picked = jnp.where(index == where[k], apart, 0.0)
                found[k] = found[k] + jnp.sum(picked, axis=0, keepdims=True)
        for k in range(3):
            anchors_ref[k : k + 1, lanes] = (found[k] + SLACK_GAP) * BASE2
            anchors_ref[3 + k : 4 + k, lanes] = where[k].astype(f32)
        weight = meta[8:9, :] + meta[9:10, :] + meta[10:11, :]
        anchors_ref[6:7, lanes] = weight * scale
        anchors_ref[7:8, lanes] = meta[0:1, :] * 128.0 + meta[1:2, :]
    sums_ref[...] = jnp.zeros_like(sums_ref)
    for offset, p, coef_ref, grad_ref in ((0, p0, c0, grad0), (2, n2, c2, grad2)):
        score_negatives(
            offset, scal_ref, p, tile, anchors_ref, coef_ref, sums_ref, grad_ref, products_ref,
            lanes_ref, sq_ref, label_ref,
        )


def last_kernel(
    scal_ref, n1, n2, p0, p1, p2, p3, c0, c2, anchors_ref, before_ref, sums_ref, grad_ref,
    keep0, send1, keep2, send3, coef_ref, products_ref, lanes_ref, sq_ref, label_ref,
):
    n = p0.shape[0] - META
    tile = [p[:n, :] for p in (p0, p1, p2, p3)]
    sums_ref[...] = before_ref[...]
    score_negatives(
        1, scal_ref, n1, tile, anchors_ref, coef_ref, sums_ref, grad_ref, products_ref,
        lanes_ref, sq_ref, label_ref,
    )
    for k in range(3):
        sums_ref[k : k + 1, :] = sums_ref[k : k + 1, :] * anchors_ref[6:7, :]
    for i, ref in enumerate((keep0, send1, keep2, send3)):
        lanes = slice(i * n, (i + 1) * n)
        total = tn(c0[:, lanes], p0[:n, :])
        total = total + tn(coef_ref[:, lanes], n1[:n, :]) + tn(c2[:, lanes], n2[:n, :])
        ref[...] = 2.0 * total


def halved_kernel(keep_ref, other_ref, out_ref):
    out_ref[...] = (keep_ref[...] + other_ref[...]).astype(bf16)


def listed_kernel(
    anchors_ref, s0, s1, s2, s3, p0, p1, p2, p3, keep_ref, other_ref, own_ref, out_ref, loss_ref
):
    n = p0.shape[0] - META
    tile = [p[:n, :] for p in (p0, p1, p2, p3)]
    sums = []
    for i in range(4):
        parts = [s[:, (i ^ j) * n : ((i ^ j) + 1) * n] for j, s in enumerate((s0, s1, s2, s3))]
        sums.append((parts[0] + parts[1]) + (parts[2] + parts[3]))
    loss_ref[...] = sums[0][3:4, :] * (1.0 / (SMOOTHING_SCALE * 3 * 4 * n))
    own_coef = [column(sums[0][k : k + 1, :]) for k in range(3)]
    own_where = [column(anchors_ref[3 + k : 4 + k, :n]) for k in range(3)]
    total = jnp.zeros(out_ref.shape, f32)
    pushed = jnp.zeros((n, 1), f32)
    for i, part in enumerate(tile):
        lanes = slice(i * n, (i + 1) * n)
        mine = lax.broadcasted_iota(jnp.int32, (n, n), 0).astype(f32)
        others = (lax.broadcasted_iota(jnp.int32, (n, n), 1) + i * n).astype(f32)
        matrix = jnp.zeros((n, n), f32)
        for k in range(3):
            hit = anchors_ref[3 + k : 4 + k, lanes] == mine
            matrix = matrix + jnp.where(hit, sums[i][k : k + 1, :], 0.0)
        pushed = pushed + jnp.sum(matrix, axis=1, keepdims=True)
        for k in range(3):
            matrix = matrix + jnp.where(own_where[k] == others, own_coef[k], 0.0)
        high = matrix.astype(bf16)
        low = (matrix - high.astype(f32)).astype(bf16)
        total = total + nn(high, part) + nn(low, part)
    base = keep_ref[...] + other_ref[...] + own_ref[...]
    out_ref[...] = base + 2.0 * (pushed * tile[0].astype(f32) - total)


def gathered_kernel(base_ref, y_ref, one_ref, two_ref, out_ref):
    total = base_ref[...] + y_ref[...].astype(f32)
    out_ref[...] = (total + (one_ref[...].astype(f32) + two_ref[...].astype(f32))).astype(bf16)


def chosen_kernel(scal_ref, own_ref, other_ref, out_ref):
    out_ref[...] = jnp.where(scal_ref[4] > 0, other_ref[...], own_ref[...])


def head_kernel(f0, f1, f2, f3, g0, g1, g2, g3, out_ref):
    total = nn(f0[...], g0[...]) + nn(f1[...], g1[...])
    total = total + nn(f2[...], g2[...]) + nn(f3[...], g3[...])
    out_ref[...] = total.astype(bf16)


def local(features, head_weight, labels, pos_index, pair_mask, loss_weight):
    blks, rows_n = lax.axis_size("blk"), lax.axis_size("rows")
    me = lax.axis_index("rows")
    n, depth = features.shape
    wide = head_weight.shape[1]
    slice_rows = depth // (blks * rows_n)

    def over_rows(x, flip):
        return lax.ppermute(x, "rows", [(i, i ^ flip) for i in range(rows_n)])

    def two_on(x, by):
        return lax.ppermute(x, "blk", [(b, (b + by) % blks) for b in range(blks)])

    def swapped(x):
        pairs = [
            (b * rows_n + i, (b ^ 1) * rows_n + (i ^ 2)) for b in range(blks) for i in range(rows_n)
        ]
        return lax.ppermute(x, ("blk", "rows"), pairs)

    def one_back(x):
        pairs = [
            (b * rows_n + i, (b - 1) % blks * rows_n + (i ^ 2))
            for b in range(blks)
            for i in range(rows_n)
        ]
        return lax.ppermute(x, ("blk", "rows"), pairs)

    odd = lax.axis_index("blk") % 2
    scal = jnp.concatenate([me[None], pair_mask[0], odd[None]]).astype(jnp.int32)
    p0 = embed(features, head_weight, labels[None], pos_index.T, loss_weight[None])
    p2 = over_rows(p0, 2)
    n2 = two_on(p0, 2)
    p1 = over_rows(p0, 1)

    features, _ = lax.optimization_barrier((features, p0))
    m = blks * slice_rows
    turned = features.T.reshape(blks, rows_n, slice_rows, n)
    turned = [
        lax.dynamic_index_in_dim(turned, me ^ j, 1, keepdims=False).reshape(m, n) for j in range(4)
    ]
    f0 = turned[0]
    p2, *turned = lax.optimization_barrier((p2, *turned))
    p3 = over_rows(p2, 1)
    f1 = over_rows(turned[1], 1)
    f2, f3 = over_rows(turned[2], 2), over_rows(turned[3], 2)

    (chosen,) = call(
        chosen_kernel,
        (scal, p0, n2),
        [shape(n + META, wide, dtype=bf16)],
        name="row_choice",
    )
    n1 = swapped(chosen)
    scratch = [pltpu.VMEM((n, n), f32)] + [pltpu.VMEM((n, 128), f32)] * 3
    tile = (p0, p1, p2, p3)
    low_grad = shape(n, wide, dtype=bf16)
    low_coef = shape(n, 4 * n, dtype=bf16)
    anchors, c0, c2, sums, own_grad, grad2 = call(
        own_kernel,
        (scal, *tile, n2),
        [shape(8, 4 * n), low_coef, low_coef, shape(8, 4 * n), shape(n, wide), low_grad],
        scratch,
        name="own_and_two_before",
    )
    grad2, f1, f2, f3 = lax.optimization_barrier((grad2, f1, f2, f3))
    grad2 = two_on(grad2, -2)
    s0, grad1, keep0, send1, keep2, send3 = call(
        last_kernel,
        (scal, n1, n2, *tile, c0, c2, anchors, sums),
        [shape(8, 4 * n), low_grad] + [shape(n, wide)] * 4,
        [pltpu.VMEM((n, 4 * n), bf16), *scratch],
        name="block_before",
    )
    grad1 = one_back(grad1)
    s2 = over_rows(s0, 2)
    s1 = over_rows(s0, 1)
    send3, grad2 = lax.optimization_barrier((send3, grad2))
    other3 = over_rows(send3, 1)
    keep2, s2 = lax.optimization_barrier((keep2, s2))
    (half,) = call(halved_kernel, (keep2, other3), [low_grad], name="half_sum")
    from_y = over_rows(half, 2)
    f3, s3 = over_rows(f3, 1), over_rows(s2, 1)
    s1, s3, f3 = lax.optimization_barrier((s1, s3, f3))
    base, anchor_loss = call(
        listed_kernel,
        (anchors, s0, s1, s2, s3, *tile, keep0, over_rows(send1, 1), own_grad),
        [shape(n, wide), shape(1, n)],
        name="listed",
    )
    (g0,) = call(
        gathered_kernel, (base, from_y, grad1, grad2), [low_grad], name="row_grad"
    )
    g2 = over_rows(g0, 2)
    g1 = over_rows(g0, 1)
    g3 = over_rows(g2, 1)
    (part,) = call(
        head_kernel,
        (f0, f1, f2, f3, g0, g1, g2, g3),
        [shape(m, wide, dtype=bf16)],
        name="head_grad",
    )
    parts = lax.all_to_all(part, "blk", split_axis=0, concat_axis=0, tiled=True)
    weight_grad = jnp.sum(parts.reshape(blks, slice_rows, wide).astype(f32), axis=0)
    return anchor_loss[0], weight_grad


def solution(mesh):
    return jax.shard_map(
        local,
        mesh=mesh,
        in_specs=(
            P(("blk", "rows"), None),
            P(),
            P(("blk", "rows")),
            P(("blk", "rows"), None),
            P("blk", None),
            P(("blk", "rows")),
        ),
        out_specs=(P(("blk", "rows")), P(("blk", "rows"), None)),
        check_vma=False,
    )
```

```python
import functools

import jax
import jax.numpy as jnp
from jax import lax
from jax.experimental import pallas as pl
from jax.experimental.pallas import tpu as pltpu
from jax.sharding import PartitionSpec as P

SMOOTHING_SCALE = 16.0
SLACK_GAP = 0.1
LN2 = 0.6931471805599453
BASE2 = SMOOTHING_SCALE / LN2
MASKED = 1e30
META = 16
CHUNK = 16
f32 = jnp.float32
bf16 = jnp.bfloat16

VMEM = pl.BlockSpec(memory_space=pltpu.VMEM)
SMEM = pl.BlockSpec(memory_space=pltpu.SMEM)


def call(kernel, inputs, outs, scratch=(), flops=1 << 20, name=None):
    return pl.pallas_call(
        kernel,
        out_shape=outs,
        in_specs=[SMEM if x.ndim == 1 else VMEM for x in inputs],
        out_specs=[VMEM] * len(outs),
        scratch_shapes=list(scratch),
        compiler_params=pltpu.CompilerParams(vmem_limit_bytes=16 << 20),
        cost_estimate=pl.CostEstimate(
            flops=flops, bytes_accessed=1024, transcendentals=0
        ),
        name=name,
    )(*inputs)


def shape(*dims, dtype=f32):
    return jax.ShapeDtypeStruct(dims, dtype)


def nn(a, b):
    return jnp.dot(a, b, preferred_element_type=f32)


def nt(a, b):
    return lax.dot_general(a, b, (((1,), (1,)), ((), ())), preferred_element_type=f32)


def tn(a, b):
    return lax.dot_general(a, b, (((0,), (0,)), ((), ())), preferred_element_type=f32)


def embed_kernel(features_ref, weight_ref, labels_ref, pos_ref, loss_weight_ref, out_ref):
    n, width = features_ref.shape[0], weight_ref.shape[1]
    out_ref[:n, :] = nn(features_ref[...], weight_ref[...]).astype(bf16)
    out_ref[n:, :] = jnp.zeros((META, width), bf16)

    @pl.when(pl.program_id(0) == 0)
    def _():
        labels, pos, weight = labels_ref[...], pos_ref[...], loss_weight_ref[...]
        high = weight.astype(bf16).astype(f32)
        middle = (weight - high).astype(bf16).astype(f32)
        rows = [labels >> 7, labels & 127, pos // n, pos % n]
        rows = [x.astype(f32) for x in rows] + [high, middle, weight - high - middle]
        rows.append(jnp.zeros((META - 11, n), f32))
        out_ref[n:, :n] = jnp.concatenate(rows, axis=0).astype(bf16)


def embed(features, head_weight, labels, pos, loss_weight):
    n, depth = features.shape
    wide = head_weight.shape[1]
    step = wide // 2
    return pl.pallas_call(
        embed_kernel,
        grid=(wide // step,),
        out_shape=shape(n + META, wide, dtype=bf16),
        in_specs=[
            pl.BlockSpec((n, depth), lambda i: (0, 0)),
            pl.BlockSpec((depth, step), lambda i: (0, i)),
            pl.BlockSpec((1, n), lambda i: (0, 0)),
            pl.BlockSpec((3, n), lambda i: (0, 0)),
            pl.BlockSpec((1, n), lambda i: (0, 0)),
        ],
        out_specs=pl.BlockSpec((n + META, step), lambda i: (0, i)),
        compiler_params=pltpu.CompilerParams(vmem_limit_bytes=56 << 20),
        cost_estimate=pl.CostEstimate(flops=1 << 30, bytes_accessed=1 << 22, transcendentals=0),
        name="embed",
    )(features, head_weight, labels, pos, loss_weight)


def across(x, width):
    return jnp.concatenate([x] * (width // x.shape[1]), axis=1)


def score_block(
    rows_n, listed, tile, anchors_ref, labels_n, products_ref, coef_ref, lanes_ref, sq_ref,
    sums_ref,
):
    n = rows_n.shape[0]
    wide = rows_n.astype(f32)
    squares = jnp.sum(wide * wide, axis=1, keepdims=True) * BASE2
    sq_ref[...] = jnp.broadcast_to(jnp.where(listed, squares, MASKED), sq_ref.shape)
    lanes_ref[...] = jnp.zeros_like(lanes_ref)
    for i, part in enumerate(tile):
        lanes = slice(i * n, (i + 1) * n)
        products_ref[...] = nt(rows_n, part) * (2.0 * BASE2)
        base = [anchors_ref[k : k + 1, lanes] for k in range(3)]
        weight = anchors_ref[6:7, lanes]
        labels_a = anchors_ref[7:8, lanes]

        def step(c, carry, lanes=lanes, base=base, weight=weight, labels_a=labels_a):
            at = pl.multiple_of(c * CHUNK, CHUNK)
            rows = pl.ds(at, CHUNK)
            q = across(sq_ref[rows, :], n) - products_ref[rows, :]
            q = jnp.where(across(labels_n[rows, :], n) == labels_a, MASKED, q)
            y = [b - q for b in base]
            e = [jnp.exp2(-jnp.abs(v)) for v in y]
            a = [1.0 + v for v in e]
            a01 = a[0] * a[1]
            excess = e[0] + e[1] * a[0] + e[2] * a01
            total = 1.0 + excess
            inverse = 1.0 / total
            log_sum = jnp.log(total) + (excess - (total - 1.0))
            tops = jnp.maximum(y[0], 0.0) + jnp.maximum(y[1], 0.0) + jnp.maximum(y[2], 0.0)
            loss = tops * LN2 + log_sum
            inv2 = inverse * a[2]
            s = [inv2 * a[1], inv2 * a[0], inverse * a01]
            s = [v * jnp.where(w >= 0.0, 1.0, x) for v, w, x in zip(s, y, e)]
            coef = (s[0] + s[1] + s[2]) * weight
            coef_ref[rows, lanes] = coef.astype(bf16)
            folded = coef[:, :128]
            for j in range(128, n, 128):
                folded = folded + coef[:, j : j + 128]
            lanes_ref[rows, :] += folded
            fold = lambda v: jnp.sum(v.reshape(CHUNK // 8, 8, n), axis=0)
            return tuple(x + fold(v) for x, v in zip(carry, (*s, loss)))

        zero = jnp.zeros((8, n), f32)
        sums = lax.fori_loop(0, n // CHUNK, step, (zero,) * 4, unroll=n // CHUNK)
        for k, v in enumerate(sums):
            sums_ref[k : k + 1, lanes] += jnp.sum(v, axis=0, keepdims=True)


def negative_grad(rows_n, tile, coef_ref, lanes_ref):
    n = rows_n.shape[0]
    pulled = sum(nn(coef_ref[:, i * n : (i + 1) * n], part) for i, part in enumerate(tile))
    col_sums = jnp.sum(lanes_ref[...], axis=1, keepdims=True)
    return 2.0 * (pulled - col_sums * rows_n.astype(f32))


def column(row):
    n = row.shape[1]
    eye = lax.broadcasted_iota(jnp.int32, (n, n), 0) == lax.broadcasted_iota(jnp.int32, (n, n), 1)
    return jnp.sum(jnp.where(eye, jnp.broadcast_to(row, (n, n)), 0.0), axis=1, keepdims=True)


def meta_row(ref, n, i):
    return ref[n : n + META, :n].astype(f32)[i : i + 1, :]


def score_negatives(
    offset, scal_ref, p, tile, anchors_ref, coef_ref, sums_ref, grad_ref, products_ref, lanes_ref,
    sq_ref, label_ref,
):
    n = p.shape[0] - META
    labels = meta_row(p, n, 0) * 128.0 + meta_row(p, n, 1)
    label_ref[...] = jnp.broadcast_to(column(labels), label_ref.shape)
    rows_n = p[:n, :]
    score_block(
        rows_n, scal_ref[1 + offset] > 0, tile, anchors_ref, label_ref, products_ref, coef_ref,
        lanes_ref, sq_ref, sums_ref,
    )
    grad_ref[...] = negative_grad(rows_n, tile, coef_ref, lanes_ref).astype(grad_ref.dtype)


def own_kernel(
    scal_ref, p0, p1, p2, p3, n2, anchors_ref, c0, c2, sums_ref, grad0, grad2,
    products_ref, lanes_ref, sq_ref, label_ref,
):
    blocks = (p0, p1, p2, p3)
    n = p0.shape[0] - META
    me = scal_ref[0]
    scale = 1.0 / (3 * 4 * n)
    tile = [p[:n, :] for p in blocks]
    squares = []
    for part in tile:
        wide = part.astype(f32)
        squares.append(jnp.sum(wide * wide, axis=1, keepdims=True))
    for i, p in enumerate(blocks):
        lanes = slice(i * n, (i + 1) * n)
        meta = p[n : n + META, :n].astype(f32)
        where = []
        for k in range(3):
            holder = meta[2 + k : 3 + k, :].astype(jnp.int32) ^ me
            where.append(holder * n + meta[5 + k : 6 + k, :].astype(jnp.int32))
        found = [jnp.zeros((1, n), f32) for _ in range(3)]
        for j, part in enumerate(tile):
            apart = squares[j] - 2.0 * nt(part, tile[i])
            index = lax.broadcasted_iota(jnp.int32, (n, n), 0) + j * n
            for k in range(3):
                picked = jnp.where(index == where[k], apart, 0.0)
                found[k] = found[k] + jnp.sum(picked, axis=0, keepdims=True)
        for k in range(3):
            anchors_ref[k : k + 1, lanes] = (found[k] + SLACK_GAP) * BASE2
            anchors_ref[3 + k : 4 + k, lanes] = where[k].astype(f32)
        weight = meta[8:9, :] + meta[9:10, :] + meta[10:11, :]
        anchors_ref[6:7, lanes] = weight * scale
        anchors_ref[7:8, lanes] = meta[0:1, :] * 128.0 + meta[1:2, :]
    sums_ref[...] = jnp.zeros_like(sums_ref)
    for offset, p, coef_ref, grad_ref in ((0, p0, c0, grad0), (2, n2, c2, grad2)):
        score_negatives(
            offset, scal_ref, p, tile, anchors_ref, coef_ref, sums_ref, grad_ref, products_ref,
            lanes_ref, sq_ref, label_ref,
        )


def last_kernel(
    scal_ref, n1, n2, p0, p1, p2, p3, c0, c2, anchors_ref, before_ref, sums_ref, grad_ref,
    keep0, send1, keep2, send3, coef_ref, products_ref, lanes_ref, sq_ref, label_ref,
):
    n = p0.shape[0] - META
    tile = [p[:n, :] for p in (p0, p1, p2, p3)]
    sums_ref[...] = before_ref[...]
    score_negatives(
        1, scal_ref, n1, tile, anchors_ref, coef_ref, sums_ref, grad_ref, products_ref,
        lanes_ref, sq_ref, label_ref,
    )
    for k in range(3):
        sums_ref[k : k + 1, :] = sums_ref[k : k + 1, :] * anchors_ref[6:7, :]
    for i, ref in enumerate((keep0, send1, keep2, send3)):
        lanes = slice(i * n, (i + 1) * n)
        total = tn(c0[:, lanes], p0[:n, :])
        total = total + tn(coef_ref[:, lanes], n1[:n, :]) + tn(c2[:, lanes], n2[:n, :])
        ref[...] = 2.0 * total


def halved_kernel(keep_ref, other_ref, out_ref):
    out_ref[...] = (keep_ref[...] + other_ref[...]).astype(bf16)


def listed_kernel(
    anchors_ref, s0, s1, s2, s3, p0, p1, p2, p3, keep_ref, other_ref, own_ref, out_ref, loss_ref
):
    n = p0.shape[0] - META
    tile = [p[:n, :] for p in (p0, p1, p2, p3)]
    sums = []
    for i in range(4):
        parts = [s[:, (i ^ j) * n : ((i ^ j) + 1) * n] for j, s in enumerate((s0, s1, s2, s3))]
        sums.append((parts[0] + parts[1]) + (parts[2] + parts[3]))
    loss_ref[...] = sums[0][3:4, :] * (1.0 / (SMOOTHING_SCALE * 3 * 4 * n))
    own_coef = [column(sums[0][k : k + 1, :]) for k in range(3)]
    own_where = [column(anchors_ref[3 + k : 4 + k, :n]) for k in range(3)]
    total = jnp.zeros(out_ref.shape, f32)
    pushed = jnp.zeros((n, 1), f32)
    for i, part in enumerate(tile):
        lanes = slice(i * n, (i + 1) * n)
        mine = lax.broadcasted_iota(jnp.int32, (n, n), 0).astype(f32)
        others = (lax.broadcasted_iota(jnp.int32, (n, n), 1) + i * n).astype(f32)
        matrix = jnp.zeros((n, n), f32)
        for k in range(3):
            hit = anchors_ref[3 + k : 4 + k, lanes] == mine
            matrix = matrix + jnp.where(hit, sums[i][k : k + 1, :], 0.0)
        pushed = pushed + jnp.sum(matrix, axis=1, keepdims=True)
        for k in range(3):
            matrix = matrix + jnp.where(own_where[k] == others, own_coef[k], 0.0)
        high = matrix.astype(bf16)
        low = (matrix - high.astype(f32)).astype(bf16)
        total = total + nn(high, part) + nn(low, part)
    base = keep_ref[...] + other_ref[...] + own_ref[...]
    out_ref[...] = base + 2.0 * (pushed * tile[0].astype(f32) - total)


def joined_kernel(base_ref, one_ref, two_ref, out_ref):
    out_ref[...] = base_ref[...] + (one_ref[...].astype(f32) + two_ref[...].astype(f32))


def gathered_kernel(base_ref, y_ref, out_ref):
    out_ref[...] = (base_ref[...] + y_ref[...].astype(f32)).astype(bf16)


def chosen_kernel(scal_ref, own_ref, other_ref, out_ref):
    out_ref[...] = jnp.where(scal_ref[4] > 0, other_ref[...], own_ref[...])


def head_kernel(f0, f1, f2, f3, g0, g1, g2, g3, out_ref):
    total = nn(f0[...], g0[...]) + nn(f1[...], g1[...])
    total = total + nn(f2[...], g2[...]) + nn(f3[...], g3[...])
    out_ref[...] = total.astype(bf16)


def local(features, head_weight, labels, pos_index, pair_mask, loss_weight):
    blks, rows_n = lax.axis_size("blk"), lax.axis_size("rows")
    me = lax.axis_index("rows")
    n, depth = features.shape
    wide = head_weight.shape[1]
    slice_rows = depth // (blks * rows_n)

    def over_rows(x, flip):
        return lax.ppermute(x, "rows", [(i, i ^ flip) for i in range(rows_n)])

    def two_on(x, by):
        return lax.ppermute(x, "blk", [(b, (b + by) % blks) for b in range(blks)])

    def swapped(x):
        pairs = [
            (b * rows_n + i, (b ^ 1) * rows_n + (i ^ 2)) for b in range(blks) for i in range(rows_n)
        ]
        return lax.ppermute(x, ("blk", "rows"), pairs)

    def one_back(x):
        pairs = [
            (b * rows_n + i, (b - 1) % blks * rows_n + (i ^ 2))
            for b in range(blks)
            for i in range(rows_n)
        ]
        return lax.ppermute(x, ("blk", "rows"), pairs)

    odd = lax.axis_index("blk") % 2
    scal = jnp.concatenate([me[None], pair_mask[0], odd[None]]).astype(jnp.int32)
    p0 = embed(features, head_weight, labels[None], pos_index.T, loss_weight[None])
    p2 = over_rows(p0, 2)
    n2 = two_on(p0, 2)
    p1 = over_rows(p0, 1)

    features, _ = lax.optimization_barrier((features, p0))
    m = blks * slice_rows
    turned = features.T.reshape(blks, rows_n, slice_rows, n)
    turned = [
        lax.dynamic_index_in_dim(turned, me ^ j, 1, keepdims=False).reshape(m, n) for j in range(4)
    ]
    f0 = turned[0]
    p2, *turned = lax.optimization_barrier((p2, *turned))
    p3 = over_rows(p2, 1)
    f1 = over_rows(turned[1], 1)
    f2, f3 = over_rows(turned[2], 2), over_rows(turned[3], 2)

    (chosen,) = call(
        chosen_kernel,
        (scal, p0, n2),
        [shape(n + META, wide, dtype=bf16)],
        name="row_choice",
    )
    n1 = swapped(chosen)
    scratch = [pltpu.VMEM((n, n), f32)] + [pltpu.VMEM((n, 128), f32)] * 3
    tile = (p0, p1, p2, p3)
    low_grad = shape(n, wide, dtype=bf16)
    low_coef = shape(n, 4 * n, dtype=bf16)
    anchors, c0, c2, sums, own_grad, grad2 = call(
        own_kernel,
        (scal, *tile, n2),
        [shape(8, 4 * n), low_coef, low_coef, shape(8, 4 * n), shape(n, wide), low_grad],
        scratch,
        name="own_and_two_before",
    )
    grad2, f1, f2, f3 = lax.optimization_barrier((grad2, f1, f2, f3))
    grad2 = two_on(grad2, -2)
    s0, grad1, keep0, send1, keep2, send3 = call(
        last_kernel,
        (scal, n1, n2, *tile, c0, c2, anchors, sums),
        [shape(8, 4 * n), low_grad] + [shape(n, wide)] * 4,
        [pltpu.VMEM((n, 4 * n), bf16), *scratch],
        name="block_before",
    )
    grad1 = one_back(grad1)
    s2 = over_rows(s0, 2)
    s1 = over_rows(s0, 1)
    send3, grad2 = lax.optimization_barrier((send3, grad2))
    other3 = over_rows(send3, 1)
    keep2, s2 = lax.optimization_barrier((keep2, s2))
    (half,) = call(halved_kernel, (keep2, other3), [low_grad], name="half_sum")
    own_grad, half = lax.optimization_barrier((own_grad, half))
    from_y = over_rows(half, 2)
    f3, s3 = over_rows(f3, 1), over_rows(s2, 1)
    s1, s3, f3 = lax.optimization_barrier((s1, s3, f3))
    base, anchor_loss = call(
        listed_kernel,
        (anchors, s0, s1, s2, s3, *tile, keep0, over_rows(send1, 1), own_grad),
        [shape(n, wide), shape(1, n)],
        name="listed",
    )
    (base,) = call(
        joined_kernel, (base, grad1, grad2), [shape(n, wide)], flops=1 << 31, name="joined"
    )
    (g0,) = call(gathered_kernel, (base, from_y), [low_grad], name="row_grad")
    g2 = over_rows(g0, 2)
    g1 = over_rows(g0, 1)
    g3 = over_rows(g2, 1)
    (part,) = call(
        head_kernel,
        (f0, f1, f2, f3, g0, g1, g2, g3),
        [shape(m, wide, dtype=bf16)],
        name="head_grad",
    )
    parts = lax.all_to_all(part, "blk", split_axis=0, concat_axis=0, tiled=True)
    weight_grad = jnp.sum(parts.reshape(blks, slice_rows, wide).astype(f32), axis=0)
    return anchor_loss[0], weight_grad


def solution(mesh):
    return jax.shard_map(
        local,
        mesh=mesh,
        in_specs=(
            P(("blk", "rows"), None),
            P(),
            P(("blk", "rows")),
            P(("blk", "rows"), None),
            P("blk", None),
            P(("blk", "rows")),
        ),
        out_specs=(P(("blk", "rows")), P(("blk", "rows"), None)),
        check_vma=False,
    )
```

```python
import functools

import jax
import jax.numpy as jnp
from jax import lax
from jax.experimental import pallas as pl
from jax.experimental.pallas import tpu as pltpu
from jax.sharding import PartitionSpec as P

SMOOTHING_SCALE = 16.0
SLACK_GAP = 0.1
LN2 = 0.6931471805599453
BASE2 = SMOOTHING_SCALE / LN2
MASKED = 1e30
META = 16
CHUNK = 16
f32 = jnp.float32
bf16 = jnp.bfloat16

VMEM = pl.BlockSpec(memory_space=pltpu.VMEM)
SMEM = pl.BlockSpec(memory_space=pltpu.SMEM)


def call(kernel, inputs, outs, scratch=(), flops=1 << 20, name=None):
    return pl.pallas_call(
        kernel,
        out_shape=outs,
        in_specs=[SMEM if x.ndim == 1 else VMEM for x in inputs],
        out_specs=[VMEM] * len(outs),
        scratch_shapes=list(scratch),
        compiler_params=pltpu.CompilerParams(vmem_limit_bytes=16 << 20),
        cost_estimate=pl.CostEstimate(
            flops=flops, bytes_accessed=1024, transcendentals=0
        ),
        name=name,
    )(*inputs)


def shape(*dims, dtype=f32):
    return jax.ShapeDtypeStruct(dims, dtype)


def nn(a, b):
    return jnp.dot(a, b, preferred_element_type=f32)


def nt(a, b):
    return lax.dot_general(a, b, (((1,), (1,)), ((), ())), preferred_element_type=f32)


def tn(a, b):
    return lax.dot_general(a, b, (((0,), (0,)), ((), ())), preferred_element_type=f32)


def embed_kernel(features_ref, weight_ref, labels_ref, pos_ref, loss_weight_ref, out_ref):
    n, width = features_ref.shape[0], weight_ref.shape[1]
    out_ref[:n, :] = nn(features_ref[...], weight_ref[...]).astype(bf16)
    out_ref[n:, :] = jnp.zeros((META, width), bf16)

    @pl.when(pl.program_id(0) == 0)
    def _():
        labels, pos, weight = labels_ref[...], pos_ref[...], loss_weight_ref[...]
        high = weight.astype(bf16).astype(f32)
        middle = (weight - high).astype(bf16).astype(f32)
        rows = [labels >> 7, labels & 127, pos // n, pos % n]
        rows = [x.astype(f32) for x in rows] + [high, middle, weight - high - middle]
        rows.append(jnp.zeros((META - 11, n), f32))
        out_ref[n:, :n] = jnp.concatenate(rows, axis=0).astype(bf16)


def embed(features, head_weight, labels, pos, loss_weight):
    n, depth = features.shape
    wide = head_weight.shape[1]
    step = wide // 2
    return pl.pallas_call(
        embed_kernel,
        grid=(wide // step,),
        out_shape=shape(n + META, wide, dtype=bf16),
        in_specs=[
            pl.BlockSpec((n, depth), lambda i: (0, 0)),
            pl.BlockSpec((depth, step), lambda i: (0, i)),
            pl.BlockSpec((1, n), lambda i: (0, 0)),
            pl.BlockSpec((3, n), lambda i: (0, 0)),
            pl.BlockSpec((1, n), lambda i: (0, 0)),
        ],
        out_specs=pl.BlockSpec((n + META, step), lambda i: (0, i)),
        compiler_params=pltpu.CompilerParams(vmem_limit_bytes=56 << 20),
        cost_estimate=pl.CostEstimate(flops=1 << 30, bytes_accessed=1 << 22, transcendentals=0),
        name="embed",
    )(features, head_weight, labels, pos, loss_weight)


def across(x, width):
    return jnp.concatenate([x] * (width // x.shape[1]), axis=1)


def score_block(
    rows_n, listed, tile, anchors_ref, labels_n, products_ref, coef_ref, lanes_ref, sq_ref,
    sums_ref,
):
    n = rows_n.shape[0]
    wide = rows_n.astype(f32)
    squares = jnp.sum(wide * wide, axis=1, keepdims=True) * BASE2
    sq_ref[...] = jnp.broadcast_to(jnp.where(listed, squares, MASKED), sq_ref.shape)
    lanes_ref[...] = jnp.zeros_like(lanes_ref)
    for i, part in enumerate(tile):
        lanes = slice(i * n, (i + 1) * n)
        products_ref[...] = nt(rows_n, part) * (2.0 * BASE2)
        base = [anchors_ref[k : k + 1, lanes] for k in range(3)]
        weight = anchors_ref[6:7, lanes]
        labels_a = anchors_ref[7:8, lanes]

        def step(c, carry, lanes=lanes, base=base, weight=weight, labels_a=labels_a):
            at = pl.multiple_of(c * CHUNK, CHUNK)
            rows = pl.ds(at, CHUNK)
            q = across(sq_ref[rows, :], n) - products_ref[rows, :]
            q = jnp.where(across(labels_n[rows, :], n) == labels_a, MASKED, q)
            y = [b - q for b in base]
            e = [jnp.exp2(-jnp.abs(v)) for v in y]
            a = [1.0 + v for v in e]
            a01 = a[0] * a[1]
            excess = e[0] + e[1] * a[0] + e[2] * a01
            total = 1.0 + excess
            inverse = 1.0 / total
            log_sum = jnp.log(total) + (excess - (total - 1.0))
            tops = jnp.maximum(y[0], 0.0) + jnp.maximum(y[1], 0.0) + jnp.maximum(y[2], 0.0)
            loss = tops * LN2 + log_sum
            inv2 = inverse * a[2]
            s = [inv2 * a[1], inv2 * a[0], inverse * a01]
            s = [v * jnp.where(w >= 0.0, 1.0, x) for v, w, x in zip(s, y, e)]
            coef = (s[0] + s[1] + s[2]) * weight
            coef_ref[rows, lanes] = coef.astype(bf16)
            folded = coef[:, :128]
            for j in range(128, n, 128):
                folded = folded + coef[:, j : j + 128]
            lanes_ref[rows, :] += folded
            fold = lambda v: jnp.sum(v.reshape(CHUNK // 8, 8, n), axis=0)
            return tuple(x + fold(v) for x, v in zip(carry, (*s, loss)))

        zero = jnp.zeros((8, n), f32)
        sums = lax.fori_loop(0, n // CHUNK, step, (zero,) * 4, unroll=n // CHUNK)
        for k, v in enumerate(sums):
            sums_ref[k : k + 1, lanes] += jnp.sum(v, axis=0, keepdims=True)


def negative_grad(rows_n, tile, coef_ref, lanes_ref):
    n = rows_n.shape[0]
    pulled = sum(nn(coef_ref[:, i * n : (i + 1) * n], part) for i, part in enumerate(tile))
    col_sums = jnp.sum(lanes_ref[...], axis=1, keepdims=True)
    return 2.0 * (pulled - col_sums * rows_n.astype(f32))


def column(row):
    n = row.shape[1]
    eye = lax.broadcasted_iota(jnp.int32, (n, n), 0) == lax.broadcasted_iota(jnp.int32, (n, n), 1)
    return jnp.sum(jnp.where(eye, jnp.broadcast_to(row, (n, n)), 0.0), axis=1, keepdims=True)


def meta_row(ref, n, i):
    return ref[n : n + META, :n].astype(f32)[i : i + 1, :]


def score_negatives(
    offset, scal_ref, p, tile, anchors_ref, coef_ref, sums_ref, grad_ref, products_ref, lanes_ref,
    sq_ref, label_ref,
):
    n = p.shape[0] - META
    labels = meta_row(p, n, 0) * 128.0 + meta_row(p, n, 1)
    label_ref[...] = jnp.broadcast_to(column(labels), label_ref.shape)
    rows_n = p[:n, :]
    score_block(
        rows_n, scal_ref[1 + offset] > 0, tile, anchors_ref, label_ref, products_ref, coef_ref,
        lanes_ref, sq_ref, sums_ref,
    )
    grad_ref[...] = negative_grad(rows_n, tile, coef_ref, lanes_ref).astype(grad_ref.dtype)


def own_kernel(
    scal_ref, p0, p1, p2, p3, n2, anchors_ref, c0, c2, sums_ref, grad0, grad2,
    products_ref, lanes_ref, sq_ref, label_ref,
):
    blocks = (p0, p1, p2, p3)
    n = p0.shape[0] - META
    me = scal_ref[0]
    scale = 1.0 / (3 * 4 * n)
    tile = [p[:n, :] for p in blocks]
    squares = []
    for part in tile:
        wide = part.astype(f32)
        squares.append(jnp.sum(wide * wide, axis=1, keepdims=True))
    for i, p in enumerate(blocks):
        lanes = slice(i * n, (i + 1) * n)
        meta = p[n : n + META, :n].astype(f32)
        where = []
        for k in range(3):
            holder = meta[2 + k : 3 + k, :].astype(jnp.int32) ^ me
            where.append(holder * n + meta[5 + k : 6 + k, :].astype(jnp.int32))
        found = [jnp.zeros((1, n), f32) for _ in range(3)]
        for j, part in enumerate(tile):
            apart = squares[j] - 2.0 * nt(part, tile[i])
            index = lax.broadcasted_iota(jnp.int32, (n, n), 0) + j * n
            for k in range(3):
                picked = jnp.where(index == where[k], apart, 0.0)
                found[k] = found[k] + jnp.sum(picked, axis=0, keepdims=True)
        for k in range(3):
            anchors_ref[k : k + 1, lanes] = (found[k] + SLACK_GAP) * BASE2
            anchors_ref[3 + k : 4 + k, lanes] = where[k].astype(f32)
        weight = meta[8:9, :] + meta[9:10, :] + meta[10:11, :]
        anchors_ref[6:7, lanes] = weight * scale
        anchors_ref[7:8, lanes] = meta[0:1, :] * 128.0 + meta[1:2, :]
    sums_ref[...] = jnp.zeros_like(sums_ref)
    for offset, p, coef_ref, grad_ref in ((0, p0, c0, grad0), (2, n2, c2, grad2)):
        score_negatives(
            offset, scal_ref, p, tile, anchors_ref, coef_ref, sums_ref, grad_ref, products_ref,
            lanes_ref, sq_ref, label_ref,
        )


def last_kernel(
    scal_ref, n1, n2, p0, p1, p2, p3, c0, c2, anchors_ref, before_ref, sums_ref, grad_ref,
    keep0, keep2, *rest
):
    sends, (coef_ref, products_ref, lanes_ref, sq_ref, label_ref) = rest[:-5], rest[-5:]
    n = p0.shape[0] - META
    tile = [p[:n, :] for p in (p0, p1, p2, p3)]
    sums_ref[...] = before_ref[...]
    score_negatives(
        1, scal_ref, n1, tile, anchors_ref, coef_ref, sums_ref, grad_ref, products_ref,
        lanes_ref, sq_ref, label_ref,
    )
    for k in range(3):
        sums_ref[k : k + 1, :] = sums_ref[k : k + 1, :] * anchors_ref[6:7, :]
    pieces = len(sends) // 2
    targets = ((keep0,), sends[:pieces], (keep2,), sends[pieces:])
    for i, refs in enumerate(targets):
        lanes = slice(i * n, (i + 1) * n)
        total = tn(c0[:, lanes], p0[:n, :])
        total = total + tn(coef_ref[:, lanes], n1[:n, :]) + tn(c2[:, lanes], n2[:n, :])
        part = n // len(refs)
        for j, ref in enumerate(refs):
            ref[...] = 2.0 * total[j * part : (j + 1) * part, :]


def halved_kernel(keep_ref, *refs):
    others, out_ref = refs[:-1], refs[-1]
    other = jnp.concatenate([x[...] for x in others], axis=0)
    out_ref[...] = (keep_ref[...] + other).astype(bf16)


def listed_kernel(
    anchors_ref, s0, s1, s2, s3, p0, p1, p2, p3, keep_ref, own_ref, *refs
):
    sent, (out_ref, loss_ref) = refs[:-2], refs[-2:]
    n = p0.shape[0] - META
    tile = [p[:n, :] for p in (p0, p1, p2, p3)]
    sums = []
    for i in range(4):
        parts = [s[:, (i ^ j) * n : ((i ^ j) + 1) * n] for j, s in enumerate((s0, s1, s2, s3))]
        sums.append((parts[0] + parts[1]) + (parts[2] + parts[3]))
    loss_ref[...] = sums[0][3:4, :] * (1.0 / (SMOOTHING_SCALE * 3 * 4 * n))
    own_coef = [column(sums[0][k : k + 1, :]) for k in range(3)]
    own_where = [column(anchors_ref[3 + k : 4 + k, :n]) for k in range(3)]
    total = jnp.zeros(out_ref.shape, f32)
    pushed = jnp.zeros((n, 1), f32)
    for i, part in enumerate(tile):
        lanes = slice(i * n, (i + 1) * n)
        mine = lax.broadcasted_iota(jnp.int32, (n, n), 0).astype(f32)
        others = (lax.broadcasted_iota(jnp.int32, (n, n), 1) + i * n).astype(f32)
        matrix = jnp.zeros((n, n), f32)
        for k in range(3):
            hit = anchors_ref[3 + k : 4 + k, lanes] == mine
            matrix = matrix + jnp.where(hit, sums[i][k : k + 1, :], 0.0)
        pushed = pushed + jnp.sum(matrix, axis=1, keepdims=True)
        for k in range(3):
            matrix = matrix + jnp.where(own_where[k] == others, own_coef[k], 0.0)
        high = matrix.astype(bf16)
        low = (matrix - high.astype(f32)).astype(bf16)
        total = total + nn(high, part) + nn(low, part)
    base = keep_ref[...] + jnp.concatenate([x[...] for x in sent], axis=0) + own_ref[...]
    out_ref[...] = base + 2.0 * (pushed * tile[0].astype(f32) - total)


def joined_kernel(base_ref, one_ref, two_ref, out_ref):
    out_ref[...] = base_ref[...] + (one_ref[...].astype(f32) + two_ref[...].astype(f32))


def gathered_kernel(base_ref, y_ref, out_ref):
    out_ref[...] = (base_ref[...] + y_ref[...].astype(f32)).astype(bf16)


def chosen_kernel(scal_ref, own_ref, other_ref, out_ref):
    out_ref[...] = jnp.where(scal_ref[4] > 0, other_ref[...], own_ref[...])


def head_kernel(f0, f1, f2, f3, g0, g1, g2, g3, out_ref):
    total = nn(f0[...], g0[...]) + nn(f1[...], g1[...])
    total = total + nn(f2[...], g2[...]) + nn(f3[...], g3[...])
    out_ref[...] = total.astype(bf16)


def local(features, head_weight, labels, pos_index, pair_mask, loss_weight):
    blks, rows_n = lax.axis_size("blk"), lax.axis_size("rows")
    me = lax.axis_index("rows")
    n, depth = features.shape
    wide = head_weight.shape[1]
    slice_rows = depth // (blks * rows_n)

    def over_rows(x, flip):
        return lax.ppermute(x, "rows", [(i, i ^ flip) for i in range(rows_n)])

    def two_on(x, by):
        return lax.ppermute(x, "blk", [(b, (b + by) % blks) for b in range(blks)])

    def swapped(x):
        pairs = [
            (b * rows_n + i, (b ^ 1) * rows_n + (i ^ 2)) for b in range(blks) for i in range(rows_n)
        ]
        return lax.ppermute(x, ("blk", "rows"), pairs)

    def one_back(x):
        pairs = [
            (b * rows_n + i, (b - 1) % blks * rows_n + (i ^ 2))
            for b in range(blks)
            for i in range(rows_n)
        ]
        return lax.ppermute(x, ("blk", "rows"), pairs)

    odd = lax.axis_index("blk") % 2
    scal = jnp.concatenate([me[None], pair_mask[0], odd[None]]).astype(jnp.int32)
    p0 = embed(features, head_weight, labels[None], pos_index.T, loss_weight[None])
    p2 = over_rows(p0, 2)
    n2 = two_on(p0, 2)
    p1 = over_rows(p0, 1)

    features, _ = lax.optimization_barrier((features, p0))
    m = blks * slice_rows
    turned = features.T.reshape(blks, rows_n, slice_rows, n)
    turned = [
        lax.dynamic_index_in_dim(turned, me ^ j, 1, keepdims=False).reshape(m, n) for j in range(4)
    ]
    f0 = turned[0]
    p2, *turned = lax.optimization_barrier((p2, *turned))
    p3 = over_rows(p2, 1)
    f1 = over_rows(turned[1], 1)
    f2, f3 = over_rows(turned[2], 2), over_rows(turned[3], 2)

    (chosen,) = call(
        chosen_kernel,
        (scal, p0, n2),
        [shape(n + META, wide, dtype=bf16)],
        name="row_choice",
    )
    n1 = swapped(chosen)
    scratch = [pltpu.VMEM((n, n), f32)] + [pltpu.VMEM((n, 128), f32)] * 3
    tile = (p0, p1, p2, p3)
    low_grad = shape(n, wide, dtype=bf16)
    low_coef = shape(n, 4 * n, dtype=bf16)
    anchors, c0, c2, sums, own_grad, grad2 = call(
        own_kernel,
        (scal, *tile, n2),
        [shape(8, 4 * n), low_coef, low_coef, shape(8, 4 * n), shape(n, wide), low_grad],
        scratch,
        name="own_and_two_before",
    )
    grad2, f1, f2, f3 = lax.optimization_barrier((grad2, f1, f2, f3))
    grad2 = two_on(grad2, -2)
    s0, grad1, keep0, keep2, *sends = call(
        last_kernel,
        (scal, n1, n2, *tile, c0, c2, anchors, sums),
        [shape(8, 4 * n), low_grad] + [shape(n, wide)] * 2 + [shape(n // 4, wide)] * 8,
        [pltpu.VMEM((n, 4 * n), bf16), *scratch],
        name="block_before",
    )
    grad1 = one_back(grad1)
    s2 = over_rows(s0, 2)
    s1 = over_rows(s0, 1)
    sends = [over_rows(x, 1) for x in sends]
    keep2, s2, grad2 = lax.optimization_barrier((keep2, s2, grad2))
    (half,) = call(halved_kernel, (keep2, *sends[4:]), [low_grad], name="half_sum")
    own_grad, half = lax.optimization_barrier((own_grad, half))
    from_y = over_rows(half, 2)
    f3, s3 = over_rows(f3, 1), over_rows(s2, 1)
    s1, s3, f3 = lax.optimization_barrier((s1, s3, f3))
    base, anchor_loss = call(
        listed_kernel,
        (anchors, s0, s1, s2, s3, *tile, keep0, own_grad, *sends[:4]),
        [shape(n, wide), shape(1, n)],
        name="listed",
    )
    (base,) = call(
        joined_kernel, (base, grad1, grad2), [shape(n, wide)], flops=1 << 31, name="joined"
    )
    (g0,) = call(gathered_kernel, (base, from_y), [low_grad], name="row_grad")
    g2 = over_rows(g0, 2)
    g1 = over_rows(g0, 1)
    g3 = over_rows(g2, 1)
    (part,) = call(
        head_kernel,
        (f0, f1, f2, f3, g0, g1, g2, g3),
        [shape(m, wide, dtype=bf16)],
        name="head_grad",
    )
    parts = lax.all_to_all(part, "blk", split_axis=0, concat_axis=0, tiled=True)
    weight_grad = jnp.sum(parts.reshape(blks, slice_rows, wide).astype(f32), axis=0)
    return anchor_loss[0], weight_grad


def solution(mesh):
    return jax.shard_map(
        local,
        mesh=mesh,
        in_specs=(
            P(("blk", "rows"), None),
            P(),
            P(("blk", "rows")),
            P(("blk", "rows"), None),
            P("blk", None),
            P(("blk", "rows")),
        ),
        out_specs=(P(("blk", "rows")), P(("blk", "rows"), None)),
        check_vma=False,
    )
```

```python
import functools

import jax
import jax.numpy as jnp
from jax import lax
from jax.experimental import pallas as pl
from jax.experimental.pallas import tpu as pltpu
from jax.sharding import PartitionSpec as P

SMOOTHING_SCALE = 16.0
SLACK_GAP = 0.1
LN2 = 0.6931471805599453
BASE2 = SMOOTHING_SCALE / LN2
MASKED = 1e30
META = 16
CHUNK = 16
f32 = jnp.float32
bf16 = jnp.bfloat16

VMEM = pl.BlockSpec(memory_space=pltpu.VMEM)
SMEM = pl.BlockSpec(memory_space=pltpu.SMEM)


def call(kernel, inputs, outs, scratch=(), flops=1 << 20, name=None):
    return pl.pallas_call(
        kernel,
        out_shape=outs,
        in_specs=[SMEM if x.ndim == 1 else VMEM for x in inputs],
        out_specs=[VMEM] * len(outs),
        scratch_shapes=list(scratch),
        compiler_params=pltpu.CompilerParams(vmem_limit_bytes=16 << 20),
        cost_estimate=pl.CostEstimate(
            flops=flops, bytes_accessed=1024, transcendentals=0
        ),
        name=name,
    )(*inputs)


def shape(*dims, dtype=f32):
    return jax.ShapeDtypeStruct(dims, dtype)


def nn(a, b):
    return jnp.dot(a, b, preferred_element_type=f32)


def nt(a, b):
    return lax.dot_general(a, b, (((1,), (1,)), ((), ())), preferred_element_type=f32)


def tn(a, b):
    return lax.dot_general(a, b, (((0,), (0,)), ((), ())), preferred_element_type=f32)


def embed_kernel(features_ref, weight_ref, labels_ref, pos_ref, loss_weight_ref, out_ref):
    n, width = features_ref.shape[0], weight_ref.shape[1]
    out_ref[:n, :] = nn(features_ref[...], weight_ref[...]).astype(bf16)
    out_ref[n:, :] = jnp.zeros((META, width), bf16)

    @pl.when(pl.program_id(0) == 0)
    def _():
        labels, pos, weight = labels_ref[...], pos_ref[...], loss_weight_ref[...]
        high = weight.astype(bf16).astype(f32)
        middle = (weight - high).astype(bf16).astype(f32)
        rows = [labels >> 7, labels & 127, pos // n, pos % n]
        rows = [x.astype(f32) for x in rows] + [high, middle, weight - high - middle]
        rows.append(jnp.zeros((META - 11, n), f32))
        out_ref[n:, :n] = jnp.concatenate(rows, axis=0).astype(bf16)


def embed(features, head_weight, labels, pos, loss_weight):
    n, depth = features.shape
    wide = head_weight.shape[1]
    step = wide // 2
    return pl.pallas_call(
        embed_kernel,
        grid=(wide // step,),
        out_shape=shape(n + META, wide, dtype=bf16),
        in_specs=[
            pl.BlockSpec((n, depth), lambda i: (0, 0)),
            pl.BlockSpec((depth, step), lambda i: (0, i)),
            pl.BlockSpec((1, n), lambda i: (0, 0)),
            pl.BlockSpec((3, n), lambda i: (0, 0)),
            pl.BlockSpec((1, n), lambda i: (0, 0)),
        ],
        out_specs=pl.BlockSpec((n + META, step), lambda i: (0, i)),
        compiler_params=pltpu.CompilerParams(vmem_limit_bytes=56 << 20),
        cost_estimate=pl.CostEstimate(flops=1 << 30, bytes_accessed=1 << 22, transcendentals=0),
        name="embed",
    )(features, head_weight, labels, pos, loss_weight)


def across(x, width):
    return jnp.concatenate([x] * (width // x.shape[1]), axis=1)


def score_block(
    rows_n, listed, tile, anchors_ref, labels_n, products_ref, coef_ref, lanes_ref, sq_ref,
    sums_ref,
):
    n = rows_n.shape[0]
    wide = rows_n.astype(f32)
    squares = jnp.sum(wide * wide, axis=1, keepdims=True) * BASE2
    sq_ref[...] = jnp.broadcast_to(jnp.where(listed, squares, MASKED), sq_ref.shape)
    lanes_ref[...] = jnp.zeros_like(lanes_ref)
    for i, part in enumerate(tile):
        lanes = slice(i * n, (i + 1) * n)
        products_ref[...] = nt(rows_n, part) * (2.0 * BASE2)
        base = [anchors_ref[k : k + 1, lanes] for k in range(3)]
        weight = anchors_ref[6:7, lanes]
        labels_a = anchors_ref[7:8, lanes]

        def step(c, carry, lanes=lanes, base=base, weight=weight, labels_a=labels_a):
            at = pl.multiple_of(c * CHUNK, CHUNK)
            rows = pl.ds(at, CHUNK)
            q = across(sq_ref[rows, :], n) - products_ref[rows, :]
            q = jnp.where(across(labels_n[rows, :], n) == labels_a, MASKED, q)
            y = [b - q for b in base]
            e = [jnp.exp2(-jnp.abs(v)) for v in y]
            a = [1.0 + v for v in e]
            a01 = a[0] * a[1]
            excess = e[0] + e[1] * a[0] + e[2] * a01
            total = 1.0 + excess
            inverse = 1.0 / total
            log_sum = jnp.log(total) + (excess - (total - 1.0))
            tops = jnp.maximum(y[0], 0.0) + jnp.maximum(y[1], 0.0) + jnp.maximum(y[2], 0.0)
            loss = tops * LN2 + log_sum
            inv2 = inverse * a[2]
            s = [inv2 * a[1], inv2 * a[0], inverse * a01]
            s = [v * jnp.where(w >= 0.0, 1.0, x) for v, w, x in zip(s, y, e)]
            coef = (s[0] + s[1] + s[2]) * weight
            coef_ref[rows, lanes] = coef.astype(bf16)
            folded = coef[:, :128]
            for j in range(128, n, 128):
                folded = folded + coef[:, j : j + 128]
            lanes_ref[rows, :] += folded
            fold = lambda v: jnp.sum(v.reshape(CHUNK // 8, 8, n), axis=0)
            return tuple(x + fold(v) for x, v in zip(carry, (*s, loss)))

        zero = jnp.zeros((8, n), f32)
        sums = lax.fori_loop(0, n // CHUNK, step, (zero,) * 4, unroll=n // CHUNK)
        for k, v in enumerate(sums):
            sums_ref[k : k + 1, lanes] += jnp.sum(v, axis=0, keepdims=True)


def negative_grad(rows_n, tile, coef_ref, lanes_ref):
    n = rows_n.shape[0]
    pulled = sum(nn(coef_ref[:, i * n : (i + 1) * n], part) for i, part in enumerate(tile))
    col_sums = jnp.sum(lanes_ref[...], axis=1, keepdims=True)
    return 2.0 * (pulled - col_sums * rows_n.astype(f32))


def column(row):
    n = row.shape[1]
    eye = lax.broadcasted_iota(jnp.int32, (n, n), 0) == lax.broadcasted_iota(jnp.int32, (n, n), 1)
    return jnp.sum(jnp.where(eye, jnp.broadcast_to(row, (n, n)), 0.0), axis=1, keepdims=True)


def meta_row(ref, n, i):
    return ref[n : n + META, :n].astype(f32)[i : i + 1, :]


def score_negatives(
    offset, scal_ref, p, tile, anchors_ref, coef_ref, sums_ref, grad_ref, products_ref, lanes_ref,
    sq_ref, label_ref,
):
    n = p.shape[0] - META
    labels = meta_row(p, n, 0) * 128.0 + meta_row(p, n, 1)
    label_ref[...] = jnp.broadcast_to(column(labels), label_ref.shape)
    rows_n = p[:n, :]
    score_block(
        rows_n, scal_ref[1 + offset] > 0, tile, anchors_ref, label_ref, products_ref, coef_ref,
        lanes_ref, sq_ref, sums_ref,
    )
    grad_ref[...] = negative_grad(rows_n, tile, coef_ref, lanes_ref).astype(grad_ref.dtype)


def own_kernel(
    scal_ref, p0, p1, p2, p3, n2, anchors_ref, c0, c2, sums_ref, grad0, grad2,
    products_ref, lanes_ref, sq_ref, label_ref,
):
    blocks = (p0, p1, p2, p3)
    n = p0.shape[0] - META
    me = scal_ref[0]
    scale = 1.0 / (3 * 4 * n)
    tile = [p[:n, :] for p in blocks]
    squares = []
    for part in tile:
        wide = part.astype(f32)
        squares.append(jnp.sum(wide * wide, axis=1, keepdims=True))
    for i, p in enumerate(blocks):
        lanes = slice(i * n, (i + 1) * n)
        meta = p[n : n + META, :n].astype(f32)
        where = []
        for k in range(3):
            holder = meta[2 + k : 3 + k, :].astype(jnp.int32) ^ me
            where.append(holder * n + meta[5 + k : 6 + k, :].astype(jnp.int32))
        found = [jnp.zeros((1, n), f32) for _ in range(3)]
        for j, part in enumerate(tile):
            apart = squares[j] - 2.0 * nt(part, tile[i])
            index = lax.broadcasted_iota(jnp.int32, (n, n), 0) + j * n
            for k in range(3):
                picked = jnp.where(index == where[k], apart, 0.0)
                found[k] = found[k] + jnp.sum(picked, axis=0, keepdims=True)
        for k in range(3):
            anchors_ref[k : k + 1, lanes] = (found[k] + SLACK_GAP) * BASE2
            anchors_ref[3 + k : 4 + k, lanes] = where[k].astype(f32)
        weight = meta[8:9, :] + meta[9:10, :] + meta[10:11, :]
        anchors_ref[6:7, lanes] = weight * scale
        anchors_ref[7:8, lanes] = meta[0:1, :] * 128.0 + meta[1:2, :]
    sums_ref[...] = jnp.zeros_like(sums_ref)
    for offset, p, coef_ref, grad_ref in ((0, p0, c0, grad0), (2, n2, c2, grad2)):
        score_negatives(
            offset, scal_ref, p, tile, anchors_ref, coef_ref, sums_ref, grad_ref, products_ref,
            lanes_ref, sq_ref, label_ref,
        )


def last_kernel(
    scal_ref, n1, n2, p0, p1, p2, p3, c0, c2, anchors_ref, before_ref, sums_ref, grad_ref,
    keep0, keep2, *rest
):
    sends, (coef_ref, products_ref, lanes_ref, sq_ref, label_ref) = rest[:-5], rest[-5:]
    n = p0.shape[0] - META
    tile = [p[:n, :] for p in (p0, p1, p2, p3)]
    sums_ref[...] = before_ref[...]
    score_negatives(
        1, scal_ref, n1, tile, anchors_ref, coef_ref, sums_ref, grad_ref, products_ref,
        lanes_ref, sq_ref, label_ref,
    )
    for k in range(3):
        sums_ref[k : k + 1, :] = sums_ref[k : k + 1, :] * anchors_ref[6:7, :]
    pieces = len(sends) // 2
    targets = ((keep0,), sends[:pieces], (keep2,), sends[pieces:])
    for i, refs in enumerate(targets):
        lanes = slice(i * n, (i + 1) * n)
        total = tn(c0[:, lanes], p0[:n, :])
        total = total + tn(coef_ref[:, lanes], n1[:n, :]) + tn(c2[:, lanes], n2[:n, :])
        part = n // len(refs)
        for j, ref in enumerate(refs):
            ref[...] = 2.0 * total[j * part : (j + 1) * part, :]


def halved_kernel(keep_ref, *refs):
    others, out_ref = refs[:-1], refs[-1]
    other = jnp.concatenate([x[...] for x in others], axis=0)
    out_ref[...] = (keep_ref[...] + other).astype(bf16)


def listed_kernel(
    anchors_ref, s0, s1, s2, s3, p0, p1, p2, p3, keep_ref, own_ref, *refs
):
    sent, (out_ref, loss_ref) = refs[:-2], refs[-2:]
    n = p0.shape[0] - META
    tile = [p[:n, :] for p in (p0, p1, p2, p3)]
    sums = []
    for i in range(4):
        parts = [s[:, (i ^ j) * n : ((i ^ j) + 1) * n] for j, s in enumerate((s0, s1, s2, s3))]
        sums.append((parts[0] + parts[1]) + (parts[2] + parts[3]))
    loss_ref[...] = sums[0][3:4, :] * (1.0 / (SMOOTHING_SCALE * 3 * 4 * n))
    own_coef = [column(sums[0][k : k + 1, :]) for k in range(3)]
    own_where = [column(anchors_ref[3 + k : 4 + k, :n]) for k in range(3)]
    total = jnp.zeros(out_ref.shape, f32)
    pushed = jnp.zeros((n, 1), f32)
    for i, part in enumerate(tile):
        lanes = slice(i * n, (i + 1) * n)
        mine = lax.broadcasted_iota(jnp.int32, (n, n), 0).astype(f32)
        others = (lax.broadcasted_iota(jnp.int32, (n, n), 1) + i * n).astype(f32)
        matrix = jnp.zeros((n, n), f32)
        for k in range(3):
            hit = anchors_ref[3 + k : 4 + k, lanes] == mine
            matrix = matrix + jnp.where(hit, sums[i][k : k + 1, :], 0.0)
        pushed = pushed + jnp.sum(matrix, axis=1, keepdims=True)
        for k in range(3):
            matrix = matrix + jnp.where(own_where[k] == others, own_coef[k], 0.0)
        high = matrix.astype(bf16)
        low = (matrix - high.astype(f32)).astype(bf16)
        total = total + nn(high, part) + nn(low, part)
    base = keep_ref[...] + jnp.concatenate([x[...] for x in sent], axis=0) + own_ref[...]
    out_ref[...] = base + 2.0 * (pushed * tile[0].astype(f32) - total)


def joined_kernel(base_ref, one_ref, two_ref, out_ref):
    out_ref[...] = base_ref[...] + (one_ref[...].astype(f32) + two_ref[...].astype(f32))


def gathered_kernel(base_ref, y_ref, out_ref):
    out_ref[...] = (base_ref[...] + y_ref[...].astype(f32)).astype(bf16)


def chosen_kernel(scal_ref, own_ref, other_ref, out_ref):
    out_ref[...] = jnp.where(scal_ref[4] > 0, other_ref[...], own_ref[...])


def head_kernel(f0, f1, f2, f3, g0, g1, g2, g3, out_ref):
    total = nn(f0[...], g0[...]) + nn(f1[...], g1[...])
    total = total + nn(f2[...], g2[...]) + nn(f3[...], g3[...])
    out_ref[...] = total.astype(bf16)


def local(features, head_weight, labels, pos_index, pair_mask, loss_weight):
    blks, rows_n = lax.axis_size("blk"), lax.axis_size("rows")
    me = lax.axis_index("rows")
    n, depth = features.shape
    wide = head_weight.shape[1]
    slice_rows = depth // (blks * rows_n)

    def over_rows(x, flip):
        return lax.ppermute(x, "rows", [(i, i ^ flip) for i in range(rows_n)])

    def two_on(x, by):
        return lax.ppermute(x, "blk", [(b, (b + by) % blks) for b in range(blks)])

    def swapped(x):
        pairs = [
            (b * rows_n + i, (b ^ 1) * rows_n + (i ^ 2)) for b in range(blks) for i in range(rows_n)
        ]
        return lax.ppermute(x, ("blk", "rows"), pairs)

    def one_back(x):
        pairs = [
            (b * rows_n + i, (b - 1) % blks * rows_n + (i ^ 2))
            for b in range(blks)
            for i in range(rows_n)
        ]
        return lax.ppermute(x, ("blk", "rows"), pairs)

    odd = lax.axis_index("blk") % 2
    scal = jnp.concatenate([me[None], pair_mask[0], odd[None]]).astype(jnp.int32)
    p0 = embed(features, head_weight, labels[None], pos_index.T, loss_weight[None])
    p2 = over_rows(p0, 2)
    n2 = two_on(p0, 2)
    p1 = over_rows(p0, 1)

    features, _ = lax.optimization_barrier((features, p0))
    m = blks * slice_rows
    turned = features.T.reshape(blks, rows_n, slice_rows, n)
    turned = [
        lax.dynamic_index_in_dim(turned, me ^ j, 1, keepdims=False).reshape(m, n) for j in range(4)
    ]
    f0 = turned[0]
    p2, *turned = lax.optimization_barrier((p2, *turned))
    p3 = over_rows(p2, 1)
    f1 = over_rows(turned[1], 1)
    f2, f3 = over_rows(turned[2], 2), over_rows(turned[3], 2)

    (chosen,) = call(
        chosen_kernel,
        (scal, p0, n2),
        [shape(n + META, wide, dtype=bf16)],
        name="row_choice",
    )
    n1 = swapped(chosen)
    scratch = [pltpu.VMEM((n, n), f32)] + [pltpu.VMEM((n, 128), f32)] * 3
    tile = (p0, p1, p2, p3)
    low_grad = shape(n, wide, dtype=bf16)
    low_coef = shape(n, 4 * n, dtype=bf16)
    anchors, c0, c2, sums, own_grad, grad2 = call(
        own_kernel,
        (scal, *tile, n2),
        [shape(8, 4 * n), low_coef, low_coef, shape(8, 4 * n), shape(n, wide), low_grad],
        scratch,
        name="own_and_two_before",
    )
    grad2, f1, f2, f3 = lax.optimization_barrier((grad2, f1, f2, f3))
    grad2 = two_on(grad2, -2)
    s0, grad1, keep0, keep2, *sends = call(
        last_kernel,
        (scal, n1, n2, *tile, c0, c2, anchors, sums),
        [shape(8, 4 * n), low_grad] + [shape(n, wide)] * 2 + [shape(n // 2, wide)] * 4,
        [pltpu.VMEM((n, 4 * n), bf16), *scratch],
        name="block_before",
    )
    grad1 = one_back(grad1)
    s2 = over_rows(s0, 2)
    s1 = over_rows(s0, 1)
    sends = [over_rows(x, 1) for x in sends]
    keep2, s2, grad2 = lax.optimization_barrier((keep2, s2, grad2))
    (half,) = call(halved_kernel, (keep2, *sends[2:]), [low_grad], name="half_sum")
    own_grad, half = lax.optimization_barrier((own_grad, half))
    from_y = over_rows(half, 2)
    f3, s3 = over_rows(f3, 1), over_rows(s2, 1)
    s1, s3, f3 = lax.optimization_barrier((s1, s3, f3))
    base, anchor_loss = call(
        listed_kernel,
        (anchors, s0, s1, s2, s3, *tile, keep0, own_grad, *sends[:2]),
        [shape(n, wide), shape(1, n)],
        name="listed",
    )
    (base,) = call(
        joined_kernel, (base, grad1, grad2), [shape(n, wide)], flops=1 << 31, name="joined"
    )
    (g0,) = call(gathered_kernel, (base, from_y), [low_grad], name="row_grad")
    g2 = over_rows(g0, 2)
    g1 = over_rows(g0, 1)
    g3 = over_rows(g2, 1)
    (part,) = call(
        head_kernel,
        (f0, f1, f2, f3, g0, g1, g2, g3),
        [shape(m, wide, dtype=bf16)],
        name="head_grad",
    )
    parts = lax.all_to_all(part, "blk", split_axis=0, concat_axis=0, tiled=True)
    weight_grad = jnp.sum(parts.reshape(blks, slice_rows, wide).astype(f32), axis=0)
    return anchor_loss[0], weight_grad


def solution(mesh):
    return jax.shard_map(
        local,
        mesh=mesh,
        in_specs=(
            P(("blk", "rows"), None),
            P(),
            P(("blk", "rows")),
            P(("blk", "rows"), None),
            P("blk", None),
            P(("blk", "rows")),
        ),
        out_specs=(P(("blk", "rows")), P(("blk", "rows"), None)),
        check_vma=False,
    )
```
